512 devices in a mesh: row: 32 (over x, z_lo, core), col: 16 (over z_hi, y).
Axes of the slice: x: 4, y: 4, z: 16 (z_hi: 4, z_lo: 4; z = z_hi * 4 + z_lo), core: 2. Of those that a mesh axis runs over, the one named last changes fastest.
Arguments:
- initial_block: float32 [64, 32768], P(None, ('row', 'col')), may hold values from -6 to 6
- matrix_tiles: float32 [32, 16, 4, 128, 128], P('row', 'col'), may hold values from -0.0625 to 0.0625
- tile_rows: int32 [32, 16, 4], P('row', 'col'), may hold values from 0 to 7
- tile_columns: int32 [32, 16, 4], P('row', 'col'), may hold values from 0 to 15
Outputs:
- basis: float32 [64, 32768], P(None, ('row', 'col'))
- rayleigh: float32 [64, 64], replicated
- residual: float32 [64, 32768], P(None, ('row', 'col'))
The draws below stay inside these ranges and needn't reach their ends.
All inputs are finite; a program needn't handle non-finite values.
Results may differ from the reference program's by a relative error of at most 0.00018.
Values sent between devices are 32-bit elements; how exact they have to be, the bound alone decides.
No kernel may reach another device: no remote copies, remote signals or barrier semaphores. Data moves between devices by JAX's collectives and lax.ppermute only.
A program may use at most 64 MiB of HBM per device.

```python
import jax
import jax.numpy as jnp
from jax import lax

M = 64
K = 64
TILE = 128
NT = 4
ITERS = 4
N = 32768
N_ROW = 32
N_COL = 16


def plant(result, stream_key, least, largest):
    longest = result.shape.index(max(result.shape))
    spots = []
    for shift in (0, 1):
        where = [jax.random.randint(jax.random.fold_in(stream_key, axis), (), 0, length) for axis, length in enumerate(result.shape)]
        where[longest] = (where[longest] + shift) % result.shape[longest]
        spots.append(tuple(where))
    return result.at[spots[0]].set(least).at[spots[1]].set(largest)


def shard_levels(stream_key, dims, pieces, smallest, largest):
    loudness, own = 1.0, jax.random.fold_in(stream_key, 6)
    for axis_at, blocks in pieces:
        steps = jnp.exp(jax.random.uniform(jax.random.fold_in(own, axis_at), (blocks,), jnp.float32, smallest / len(pieces), largest / len(pieces)))
        loudness = loudness * jnp.repeat(steps, dims[axis_at] // blocks).reshape([-1 if axis == axis_at else 1 for axis in range(len(dims))])
    return loudness


def centred(rng, shape, deviation, bound, cuts=(), held_as=jnp.bfloat16):
    drawn = jax.random.normal(rng, shape, jnp.float32) * deviation
    if len(cuts) > 0:
        drawn = shard_levels(rng, shape, cuts, -0.22, 0.18) * drawn
    return jnp.clip(drawn, min=-bound, max=bound).astype(held_as)


def setup_inputs(seed: int = 0) -> dict:
    splits = jax.random.split(jax.random.key(seed), 5)
    return {
        "initial_block": centred(splits[0], (K, N), 1.0, 6.0, ((1, 512),), jnp.float32),
        "matrix_tiles": centred(splits[1], (N_ROW, N_COL, NT, TILE, TILE), (8 * NT * TILE * TILE // M) ** -0.5, 0.0625, ((0, 32), (1, 16)), jnp.float32),
        "tile_rows": plant(jax.random.randint(splits[2], (N_ROW, N_COL, NT), 0, M * N_COL // TILE), jax.random.fold_in(splits[2], 1), 0, (M * N_COL // TILE) - 1).astype(jnp.int32),
        "tile_columns": plant(jax.random.randint(splits[3], (N_ROW, N_COL, NT), 0, M * N_ROW // TILE), jax.random.fold_in(splits[3], 1), 0, (M * N_ROW // TILE) - 1).astype(jnp.int32),
    }


step_size = 0.5
momentum = 0.4

def tile_products(row_part, column_part, device_tiles, which_rows, which_columns):
    highest = lax.Precision.HIGHEST
    block_size = row_part.shape[0]
    row_tiles = row_part.reshape(block_size, -1, TILE)
    column_tiles = column_part.reshape(block_size, -1, TILE)
    row_pick = jnp.take(row_tiles, which_rows, axis=1)
    column_pick = jnp.take(column_tiles, which_columns, axis=1)
    direct = jnp.einsum('knj,nij->kni', column_pick, device_tiles, precision=highest)
    mirrored = jnp.einsum('kni,nij->knj', row_pick, device_tiles, precision=highest)
    row_onehot = (which_rows[:, None] == jnp.arange(row_tiles.shape[1], dtype=jnp.int32)[None, :]).astype(device_tiles.dtype)
    column_onehot = (which_columns[:, None] == jnp.arange(column_tiles.shape[1], dtype=jnp.int32)[None, :]).astype(device_tiles.dtype)
    direct_sum = jnp.einsum('kni,ns->ksi', direct, row_onehot, precision=highest).reshape(block_size, -1)
    mirrored_sum = jnp.einsum('knj,ns->ksj', mirrored, column_onehot, precision=highest).reshape(block_size, -1)
    return (direct_sum, mirrored_sum)

def apply_operator(vectors, matrix_tiles, tile_rows, tile_columns):
    block_size = vectors.shape[0]
    blocked = vectors.reshape(block_size, N_ROW, N_COL, M)

    def visit(device, accumulated):
        row_index = device // N_COL
        col_index = device % N_COL
        row_part = lax.dynamic_index_in_dim(blocked, row_index, 1, False).reshape(block_size, N_COL * M)
        column_part = lax.dynamic_index_in_dim(blocked, col_index, 2, False).reshape(block_size, N_ROW * M)
        device_tiles = lax.dynamic_index_in_dim(lax.dynamic_index_in_dim(matrix_tiles, row_index, 0, False), col_index, 0, False)
        which_rows = lax.dynamic_index_in_dim(lax.dynamic_index_in_dim(tile_rows, row_index, 0, False), col_index, 0, False)
        which_columns = lax.dynamic_index_in_dim(lax.dynamic_index_in_dim(tile_columns, row_index, 0, False), col_index, 0, False)
        direct, mirrored = tile_products(row_part, column_part, device_tiles, which_rows, which_columns)
        current = lax.dynamic_index_in_dim(accumulated, row_index, 1, False)
        accumulated = lax.dynamic_update_index_in_dim(accumulated, current + direct.reshape(block_size, N_COL, M), row_index, 1)
        current = lax.dynamic_index_in_dim(accumulated, col_index, 2, False)
        accumulated = lax.dynamic_update_index_in_dim(accumulated, current + mirrored.reshape(block_size, N_ROW, M), col_index, 2)
        return accumulated
    accumulated = lax.fori_loop(0, N_ROW * N_COL, visit, jnp.zeros_like(blocked))
    return accumulated.reshape(block_size, -1)

def inverse_factor(intersection):
    factor = jnp.linalg.cholesky(intersection)
    identity = jnp.eye(intersection.shape[0], dtype=intersection.dtype)
    return jax.scipy.linalg.solve_triangular(factor, identity, lower=True)

def reference(initial_block, matrix_tiles, tile_rows, tile_columns):
    highest = lax.Precision.HIGHEST
    inverse = inverse_factor(jnp.dot(initial_block, initial_block.T, precision=highest))
    basis = jnp.dot(inverse, initial_block, precision=highest)
    image = apply_operator(basis, matrix_tiles, tile_rows, tile_columns)
    search = jnp.zeros_like(basis)
    search_image = jnp.zeros_like(basis)
    for iteration in range(ITERS):
        rayleigh = jnp.dot(basis, image.T, precision=highest)
        residual = image - jnp.dot(rayleigh, basis, precision=highest)
        residual_image = apply_operator(residual, matrix_tiles, tile_rows, tile_columns)
        search = -step_size * residual + momentum * search
        search_image = -step_size * residual_image + momentum * search_image
        trial = basis + search
        trial_image = image + search_image
        inverse = inverse_factor(jnp.dot(trial, trial.T, precision=highest))
        basis = jnp.dot(inverse, trial, precision=highest)
        image = jnp.dot(inverse, trial_image, precision=highest)
    rayleigh = jnp.dot(basis, image.T, precision=highest)
    residual = image - jnp.dot(rayleigh, basis, precision=highest)
    return (basis, rayleigh, residual)
```

```python
import functools

import jax
import jax.numpy as jnp
from jax import lax
from jax.experimental import pallas as pl
from jax.experimental.pallas import tpu as pltpu
from jax.sharding import Mesh
from jax.sharding import PartitionSpec as P

TILE = 128
HALF = 64
VEC = 64
ITERS = 4
STEP = 0.5
MOMENTUM = 0.4
AXES = ("x", "zl", "core", "zh", "y")
ROW = ("x", "zl", "core")
COL = ("zh", "y")
SPLIT = (4, 4, 2, 4, 4)


def dot(a, b, contract=((1,), (0,))):
    return lax.dot_general(
        a,
        b,
        (contract, ((), ())),
        precision=lax.Precision.HIGHEST,
        preferred_element_type=jnp.float32,
    )


NT = ((1,), (1,))


def lanes(rows):
    return lax.broadcasted_iota(jnp.int32, (rows, TILE), 1)


def swap_halves(v):
    return pltpu.roll(v, HALF, 1)


def pack_pair(tile):
    low = lanes(VEC // 2) < HALF
    top, bottom = tile[: VEC // 2], tile[VEC // 2 :]
    even = jnp.where(low, top, swap_halves(bottom))
    odd = jnp.where(low, swap_halves(top), bottom)
    return even, odd


def unpack_pair(even, odd):
    low = lanes(VEC // 2) < HALF
    top = jnp.where(low, even, swap_halves(odd))
    bottom = jnp.where(low, swap_halves(even), odd)
    return top, bottom


def inverse_cholesky(packed):
    low = lanes(VEC // 2) < HALF
    row_id = lax.broadcasted_iota(jnp.int32, (VEC // 2, TILE), 0)
    col_id = lanes(VEC // 2)
    eye_top = jnp.where(col_id - HALF == row_id, 1.0, 0.0)
    eye_bottom = jnp.where(col_id - HALF == row_id + VEC // 2, 1.0, 0.0)
    top = jnp.where(low, packed, eye_top)
    bottom = jnp.where(low, swap_halves(packed), eye_bottom)
    groups = [top[8 * g : 8 * g + 8] for g in range(4)] + [bottom[8 * g : 8 * g + 8] for g in range(4)]
    sub = lax.broadcasted_iota(jnp.int32, (8, TILE), 0)
    lane = lax.broadcasted_iota(jnp.int32, (8, TILE), 1)
    for j in range(VEC):
        own, at = divmod(j, 8)
        pivot_row = jnp.broadcast_to(groups[own][at : at + 1, :], (8, TILE))
        scale = 1.0 / jnp.broadcast_to(pivot_row[:, j : j + 1], (8, TILE))
        scaled = pivot_row * scale
        for g in range(own, 8):
            if g == own and at == 7:
                continue
            factor = jnp.broadcast_to(groups[g][:, j : j + 1], (8, TILE))
            update = groups[g] - factor * scaled
            groups[g] = jnp.where(sub > at, update, groups[g]) if g == own else update
    out = []
    for g in range(8):
        diagonal = jnp.sum(jnp.where(lane == sub + 8 * g, groups[g], 0.0), axis=1, keepdims=True)
        out.append(jnp.where(lane >= HALF, groups[g] / jnp.sqrt(diagonal), 0.0))
    return jnp.concatenate(out, axis=0)


def unpack_square(packed):
    return jnp.concatenate([packed, swap_halves(packed)], axis=0)[:, :HALF]


def small_algebra(gq_ref, size):
    gram = gq_ref[0]
    projected = unpack_square(gq_ref[1])
    right = inverse_cholesky(gram)
    left = swap_halves(right)
    inverse = left[:, :HALF]
    rayleigh = dot(dot(inverse, projected), inverse, NT)
    mixed = right - dot(rayleigh, left)
    return left, right, mixed, rayleigh


def gather_chunks(recv_row_ref, gq, count):
    each = VEC // 2 // count
    for r in range(count):
        for which in range(2):
            gq[which, r * each : (r + 1) * each, :] = recv_row_ref[
                r, VEC // 2 + which * each : VEC // 2 + (which + 1) * each, :
            ]


def emit_products(
    n_row, n_col, q, factor, own_gram, tiles_ref, rows_ref, cols_ref, send_row_ref, send_y_ref, direct, mirrored, own
):
    row_tiles, col_tiles = n_col // 2, n_row // 2
    direct[...] = jnp.zeros_like(direct)
    mirrored[...] = jnp.zeros_like(mirrored)
    cross = jnp.zeros((VEC, VEC), jnp.float32)
    for t in range(tiles_ref.shape[0]):
        i, j = rows_ref[t], cols_ref[t]
        tile = tiles_ref[t]
        row_pick = q[i]
        column_pick = q[row_tiles + j]
        product = dot(column_pick, tile, NT)
        direct[i] += product
        mirrored[j] += dot(row_pick, tile)
        cross = cross + dot(product, row_pick, NT)
    gram, projected = own_gram(own)
    projected = projected + factor * (cross + cross.T)
    low = lanes(VEC // 2) < HALF
    each = VEC // 2 // n_row

    def pack_square(m):
        wide = jnp.concatenate([m, m], axis=1)
        return jnp.where(low, wide[: VEC // 2], wide[VEC // 2 :])

    gram, projected = pack_square(gram), pack_square(projected)
    for b in range(col_tiles):
        even, odd = pack_pair(mirrored[b])
        send_row_ref[2 * b, : VEC // 2, :] = even
        send_row_ref[2 * b + 1, : VEC // 2, :] = odd
    rest = send_row_ref.shape[1] - VEC // 2 - 2 * each
    for r in range(n_row):
        pieces = [gram[r * each : (r + 1) * each], projected[r * each : (r + 1) * each]]
        if rest:
            pieces.append(jnp.zeros((rest, TILE), jnp.float32))
        send_row_ref[r, VEC // 2 :, :] = jnp.concatenate(pieces, axis=0)
    n_y = send_y_ref.shape[0]
    for s in range(row_tiles):
        for c, block in zip((2 * s, 2 * s + 1), pack_pair(direct[s])):
            zh, y = c // n_y, c % n_y
            send_y_ref[y, zh * (VEC // 2) : (zh + 1) * (VEC // 2), :] = block


def unpack_gathered(recv_row_ref, recv_col_ref, n_row, n_col, out):
    n_y = recv_col_ref.shape[0]
    half = VEC // 2

    def col_block(c):
        zh, y = c // n_y, c % n_y
        return recv_col_ref[y, zh * half : (zh + 1) * half, :]

    for s in range(n_col // 2):
        top, bottom = unpack_pair(col_block(2 * s), col_block(2 * s + 1))
        out[s, :half, :] = top
        out[s, half:, :] = bottom
    for b in range(n_row // 2):
        top, bottom = unpack_pair(recv_row_ref[2 * b, :half, :], recv_row_ref[2 * b + 1, :half, :])
        out[n_col // 2 + b, :half, :] = top
        out[n_col // 2 + b, half:, :] = bottom


def own_mask(where_ref):
    return (lanes(VEC) // HALF) == where_ref[1]


def first_kernel(
    n_row, n_col, where_ref, rows_ref, cols_ref, tiles_ref, recv_row_ref, recv_col_ref,
    trial_ref, send_row_ref, send_y_ref, direct, mirrored,
):
    unpack_gathered(recv_row_ref, recv_col_ref, n_row, n_col, trial_ref)

    def own_gram(own):
        mine = trial_ref[where_ref[0]]
        return dot(jnp.where(own_mask(where_ref), mine, 0.0), mine, NT), jnp.zeros((VEC, VEC), jnp.float32)

    emit_products(
        n_row, n_col, trial_ref, 1.0, own_gram, tiles_ref, rows_ref, cols_ref, send_row_ref, send_y_ref, direct, mirrored, None
    )


def middle_kernel(first, n_row, n_col, *refs):
    refs = list(refs)
    where_ref, rows_ref, cols_ref, tiles_ref, recv_row_ref, recv_col_ref, trial_ref = refs[:7]
    refs = refs[7:]
    if not first:
        known_ref, search_ref, search_image_ref = refs[:3]
        refs = refs[3:]
    (
        new_trial_ref, new_known_ref, new_search_ref, new_search_image_ref, send_row_ref, send_y_ref,
        direct, mirrored, fresh, gq,
    ) = refs
    n_tiles = n_col // 2 + n_row // 2
    gather_chunks(recv_row_ref, gq, n_row)
    unpack_gathered(recv_row_ref, recv_col_ref, n_row, n_col, fresh)
    left, right, mixed, _ = small_algebra(gq, n_row)
    for t in range(n_tiles):
        image = fresh[t]
        trial = trial_ref[t]
        if first:
            search = None
            trial_image = image
        else:
            search_image = -STEP * image + MOMENTUM * search_image_ref[t]
            new_search_image_ref[t] = search_image
            trial_image = known_ref[t] - STEP * image
        both = jnp.concatenate([trial, trial_image], axis=0)
        basis = dot(left, both)
        new_image = dot(right, both)
        residual = dot(mixed, both)
        fresh[t] = residual
        if first:
            new_search = -STEP * residual
            new_known_ref[t] = new_image
            new_search_image_ref[t] = jnp.zeros_like(image)
        else:
            new_search = -STEP * residual + MOMENTUM * search_ref[t]
            new_known_ref[t] = new_image + MOMENTUM * search_image
        new_search_ref[t] = new_search
        new_trial_ref[t] = basis + new_search

    def own_gram(own):
        at = where_ref[0]
        mask = own_mask(where_ref)
        trial = jnp.where(mask, new_trial_ref[at], 0.0)
        known = jnp.where(mask, new_known_ref[at], 0.0)
        gram = dot(trial, trial, NT)
        projected = dot(trial, known, NT) - STEP * dot(known, fresh[at], NT)
        return gram, projected

    emit_products(
        n_row, n_col, fresh, STEP * STEP, own_gram, tiles_ref, rows_ref, cols_ref, send_row_ref, send_y_ref,
        direct, mirrored, None,
    )


def last_kernel(n_row, where_ref, recv_ref, local_ref, trial_ref, known_ref, basis_ref, rayleigh_ref, residual_ref, gq):
    each = VEC // 2 // n_row
    for r in range(n_row):
        for which in range(2):
            gq[which, r * each : (r + 1) * each, :] = recv_ref[r, which * each : (which + 1) * each, :]
    left, right, mixed, rayleigh = small_algebra(gq, n_row)
    block = local_ref[: VEC // 2, :]
    image = jnp.concatenate(unpack_pair(block, block), axis=0)
    trial = trial_ref[where_ref[0]]
    trial_image = known_ref[where_ref[0]] - STEP * image
    both = jnp.concatenate([trial, trial_image], axis=0)
    odd = where_ref[1] == 1
    basis = dot(left, both)
    residual = dot(mixed, both)
    basis_ref[...] = jnp.where(odd, swap_halves(basis), basis)[:, :HALF]
    residual_ref[...] = jnp.where(odd, swap_halves(residual), residual)[:, :HALF]
    rayleigh_ref[...] = rayleigh


def per_device(split, initial_block, matrix_tiles, tile_rows, tile_columns):
    n_x, n_zl, n_core, n_zh, n_y = split
    n_row, n_col = n_x * n_zl * n_core, n_zh * n_y
    n_tiles = n_row // 2 + n_col // 2
    half = VEC // 2
    each = half // n_row
    extra = -(-2 * each // 8) * 8
    tiles = matrix_tiles[0, 0]
    rows, cols = tile_rows[0, 0], tile_columns[0, 0]
    my_col = lax.axis_index("zh") * n_y + lax.axis_index("y")
    where = jnp.stack([my_col // 2, my_col % 2]).astype(jnp.int32)

    smem = pl.BlockSpec(memory_space=pltpu.SMEM)
    vmem = pl.BlockSpec(memory_space=pltpu.VMEM)
    f32 = jnp.float32
    state = jax.ShapeDtypeStruct((n_tiles, VEC, TILE), f32)
    send_row = jax.ShapeDtypeStruct((n_row, half + extra, TILE), f32)
    send_y = jax.ShapeDtypeStruct((n_y, n_zh * half, TILE), f32)
    params = pltpu.CompilerParams(vmem_limit_bytes=24 * 1024 * 1024)
    partial_sums = [pltpu.VMEM((n_col // 2, VEC, TILE), f32), pltpu.VMEM((n_row // 2, VEC, TILE), f32)]

    def exchange(blocks, axes):
        return lax.all_to_all(blocks, axes, 0, 0, tiled=True)

    def spread(block, axes, count):
        return exchange(jnp.broadcast_to(block[None], (count,) + block.shape), axes)

    def scatter(row_blocks, y_blocks):
        mirrored = jnp.sum(exchange(row_blocks, ROW), axis=0)
        sums = jnp.broadcast_to(mirrored[None, half:], (n_y, extra, TILE))
        along_y = jnp.sum(exchange(jnp.concatenate([y_blocks, sums], axis=1), "y"), axis=0)
        sums = jnp.broadcast_to(along_y[None, n_zh * half :], (n_zh, extra, TILE))
        blocks = along_y[: n_zh * half].reshape(n_zh, half, TILE)
        along_z = jnp.sum(exchange(jnp.concatenate([blocks, sums], axis=1), "zh"), axis=0)
        return jnp.concatenate([along_z[:half] + mirrored[:half], along_z[half:]], axis=0)

    def gather(block):
        along_z = spread(block[:half], "zh", n_zh)
        along_y = spread(along_z.reshape(n_zh * half, TILE), "y", n_y)
        return spread(block, ROW, n_row), along_y

    start = jnp.concatenate([initial_block[:half], initial_block[half:]], axis=1)
    start = jnp.concatenate([start, jnp.zeros((extra, TILE), f32)], axis=0)
    from_row, from_col = gather(start)
    trial, row_blocks, y_blocks = pl.pallas_call(
        functools.partial(first_kernel, n_row, n_col),
        out_shape=(state, send_row, send_y),
        in_specs=[smem] * 3 + [vmem] * 3,
        out_specs=(vmem,) * 3,
        scratch_shapes=partial_sums,
        compiler_params=params,
    )(where, rows, cols, tiles, from_row, from_col)
    carried = (trial,)
    for iteration in range(ITERS):
        from_row, from_col = gather(scatter(row_blocks, y_blocks))
        *carried, row_blocks, y_blocks = pl.pallas_call(
            functools.partial(middle_kernel, iteration == 0, n_row, n_col),
            out_shape=(state,) * 4 + (send_row, send_y),
            in_specs=[smem] * 3 + [vmem] * (3 + len(carried)),
            out_specs=(vmem,) * 6,
            scratch_shapes=partial_sums
            + [pltpu.VMEM((n_tiles, VEC, TILE), f32), pltpu.VMEM((2, half, TILE), f32)],
            compiler_params=params,
        )(where, rows, cols, tiles, from_row, from_col, *carried)
    trial, known = carried[:2]
    local = scatter(row_blocks, y_blocks)
    sums = spread(local[half:], ROW, n_row)
    small = jax.ShapeDtypeStruct((VEC, VEC), f32)
    return pl.pallas_call(
        functools.partial(last_kernel, n_row),
        out_shape=(small,) * 3,
        in_specs=[smem] + [vmem] * 4,
        out_specs=(vmem,) * 3,
        scratch_shapes=[pltpu.VMEM((2, half, TILE), f32)],
        compiler_params=params,
    )(where, sums, local, trial, known)


def solution(mesh, split=SPLIT):
    fine = Mesh(mesh.devices.reshape(split), AXES)
    in_specs = (
        P(None, AXES),
        P(ROW, COL, None, None, None),
        P(ROW, COL, None),
        P(ROW, COL, None),
    )
    out_specs = (P(None, AXES), P(), P(None, AXES))
    return jax.shard_map(
        functools.partial(per_device, split),
        mesh=fine,
        in_specs=in_specs,
        out_specs=out_specs,
        check_vma=False,
    )
```

```python
import functools

import jax
import jax.numpy as jnp
from jax import lax
from jax.experimental import pallas as pl
from jax.experimental.pallas import tpu as pltpu
from jax.sharding import Mesh
from jax.sharding import PartitionSpec as P

TILE = 128
HALF = 64
VEC = 64
GROUP = 8
ITERS = 4
STEP = 0.5
MOMENTUM = 0.4
AXES = ("x", "zl", "core", "zh", "y")
ROW = ("x", "zl", "core")
CHIPS = ("x", "zl")
COL = ("zh", "y")
SPLIT = (4, 4, 2, 4, 4)


def dot(a, b, contract=((1,), (0,))):
    return lax.dot_general(
        a,
        b,
        (contract, ((), ())),
        precision=lax.Precision.HIGHEST,
        preferred_element_type=jnp.float32,
    )


NT = ((1,), (1,))


def lanes(rows):
    return lax.broadcasted_iota(jnp.int32, (rows, TILE), 1)


def swap_halves(v):
    return pltpu.roll(v, HALF, 1)


def pack_pair(tile):
    low = lanes(VEC // 2) < HALF
    top, bottom = tile[: VEC // 2], tile[VEC // 2 :]
    even = jnp.where(low, top, swap_halves(bottom))
    odd = jnp.where(low, swap_halves(top), bottom)
    return even, odd


def unpack_pair(even, odd):
    low = lanes(VEC // 2) < HALF
    top = jnp.where(low, even, swap_halves(odd))
    bottom = jnp.where(low, swap_halves(even), odd)
    return top, bottom


def inverse_cholesky(packed):
    low = lanes(VEC // 2) < HALF
    row_id = lax.broadcasted_iota(jnp.int32, (VEC // 2, TILE), 0)
    col_id = lanes(VEC // 2)
    eye_top = jnp.where(col_id - HALF == row_id, 1.0, 0.0)
    eye_bottom = jnp.where(col_id - HALF == row_id + VEC // 2, 1.0, 0.0)
    top = jnp.where(low, packed, eye_top)
    bottom = jnp.where(low, swap_halves(packed), eye_bottom)
    count = VEC // GROUP
    groups = [half[GROUP * g : GROUP * (g + 1)] for half in (top, bottom) for g in range(count // 2)]
    sub = lax.broadcasted_iota(jnp.int32, (GROUP, TILE), 0)
    lane = lanes(GROUP)

    def wide(v):
        return jnp.broadcast_to(v, (GROUP, TILE))

    out = []
    for own in range(count):
        first = own * GROUP
        columns = {
            g: [wide(groups[g][:, first + k : first + k + 1]) for k in range(GROUP)] for g in range(own, count)
        }
        rows = [wide(groups[own][k : k + 1, :]) for k in range(GROUP)]
        corner = [
            [wide(columns[own][m][k : k + 1, :]) if m >= k else None for m in range(GROUP)] for k in range(GROUP)
        ]
        scales = []
        for k in range(GROUP):
            scale = 1.0 / corner[k][k]
            scales.append(scale)
            for l in range(k + 1, GROUP):
                factor = corner[k][l] * scale
                rows[l] = rows[l] - factor * rows[k]
                for m in range(l, GROUP):
                    corner[l][m] = corner[l][m] - factor * corner[k][m]
        for g in range(own + 1, count):
            column = columns[g]
            for k in range(GROUP):
                factor = column[k] * scales[k]
                groups[g] = groups[g] - factor * rows[k]
                for m in range(k + 1, GROUP):
                    column[m] = column[m] - factor * corner[k][m]
        block, diagonal = rows[0], corner[0][0]
        for k in range(1, GROUP):
            block = jnp.where(sub == k, rows[k], block)
            diagonal = jnp.where(sub == k, corner[k][k], diagonal)
        out.append(jnp.where(lane >= HALF, block / jnp.sqrt(diagonal), 0.0))
    return jnp.concatenate(out, axis=0)


def unpack_square(packed):
    return jnp.concatenate([packed, swap_halves(packed)], axis=0)[:, :HALF]


def small_algebra(gq_ref, size):
    gram = gq_ref[0]
    projected = unpack_square(gq_ref[1])
    right = inverse_cholesky(gram)
    left = swap_halves(right)
    inverse = left[:, :HALF]
    rayleigh = dot(dot(inverse, projected), inverse, NT)
    mixed = right - dot(rayleigh, left)
    return left, right, mixed, rayleigh


def gather_chunks(recv_ref, at, gq, count):
    each = VEC // 2 // count
    for r in range(count):
        for which in range(2):
            gq[which, r * each : (r + 1) * each, :] = recv_ref[
                r % 2, r // 2, at + which * each : at + (which + 1) * each, :
            ]


def emit_products(
    n_row, n_col, q, factor, own_gram, tiles_ref, rows_ref, cols_ref, send_row_ref, send_y_ref, direct, mirrored, own
):
    row_tiles, col_tiles = n_col // 2, n_row // 2
    direct[...] = jnp.zeros_like(direct)
    mirrored[...] = jnp.zeros_like(mirrored)
    cross = jnp.zeros((VEC, VEC), jnp.float32)
    for t in range(tiles_ref.shape[0]):
        i, j = rows_ref[t], cols_ref[t]
        tile = tiles_ref[t]
        row_pick = q[i]
        column_pick = q[row_tiles + j]
        product = dot(column_pick, tile, NT)
        direct[i] += product
        mirrored[j] += dot(row_pick, tile)
        cross = cross + dot(product, row_pick, NT)
    gram, projected = own_gram(own)
    projected = projected + factor * (cross + cross.T)
    low = lanes(VEC // 2) < HALF
    each = VEC // 2 // n_row

    def pack_square(m):
        wide = jnp.concatenate([m, m], axis=1)
        return jnp.where(low, wide[: VEC // 2], wide[VEC // 2 :])

    gram, projected = pack_square(gram), pack_square(projected)
    for b in range(col_tiles):
        even, odd = pack_pair(mirrored[b])
        send_row_ref[0, b, : VEC // 2, :] = even
        send_row_ref[1, b, : VEC // 2, :] = odd
    rest = send_row_ref.shape[2] - VEC // 2 - 2 * each
    for r in range(n_row):
        pieces = [gram[r * each : (r + 1) * each], projected[r * each : (r + 1) * each]]
        if rest:
            pieces.append(jnp.zeros((rest, TILE), jnp.float32))
        send_row_ref[r % 2, r // 2, VEC // 2 :, :] = jnp.concatenate(pieces, axis=0)
    n_y = send_y_ref.shape[0]
    for s in range(row_tiles):
        for c, block in zip((2 * s, 2 * s + 1), pack_pair(direct[s])):
            zh, y = c // n_y, c % n_y
            send_y_ref[y, zh * (VEC // 2) : (zh + 1) * (VEC // 2), :] = block


def unpack_gathered(recv_row_ref, recv_col_ref, n_row, n_col, out):
    n_y = recv_col_ref.shape[0]
    half = VEC // 2

    def col_block(c):
        zh, y = c // n_y, c % n_y
        return recv_col_ref[y, zh * half : (zh + 1) * half, :]

    for s in range(n_col // 2):
        top, bottom = unpack_pair(col_block(2 * s), col_block(2 * s + 1))
        out[s, :half, :] = top
        out[s, half:, :] = bottom
    for b in range(n_row // 2):
        top, bottom = unpack_pair(recv_row_ref[0, b, :half, :], recv_row_ref[1, b, :half, :])
        out[n_col // 2 + b, :half, :] = top
        out[n_col // 2 + b, half:, :] = bottom


def own_mask(where_ref):
    return (lanes(VEC) // HALF) == where_ref[1]


def first_kernel(
    n_row, n_col, where_ref, rows_ref, cols_ref, tiles_ref, recv_row_ref, recv_col_ref,
    trial_ref, send_row_ref, send_y_ref, direct, mirrored,
):
    unpack_gathered(recv_row_ref, recv_col_ref, n_row, n_col, trial_ref)

    def own_gram(own):
        mine = trial_ref[where_ref[0]]
        return dot(jnp.where(own_mask(where_ref), mine, 0.0), mine, NT), jnp.zeros((VEC, VEC), jnp.float32)

    emit_products(
        n_row, n_col, trial_ref, 1.0, own_gram, tiles_ref, rows_ref, cols_ref, send_row_ref, send_y_ref, direct, mirrored, None
    )


def middle_kernel(first, n_row, n_col, *refs):
    refs = list(refs)
    where_ref, rows_ref, cols_ref, tiles_ref, recv_row_ref, recv_col_ref, trial_ref = refs[:7]
    refs = refs[7:]
    if not first:
        known_ref, search_ref, search_image_ref = refs[:3]
        refs = refs[3:]
    (
        new_trial_ref, new_known_ref, new_search_ref, new_search_image_ref, send_row_ref, send_y_ref,
        direct, mirrored, fresh, gq,
    ) = refs
    n_tiles = n_col // 2 + n_row // 2
    gather_chunks(recv_row_ref, VEC // 2, gq, n_row)
    unpack_gathered(recv_row_ref, recv_col_ref, n_row, n_col, fresh)
    left, right, mixed, _ = small_algebra(gq, n_row)
    for t in range(n_tiles):
        image = fresh[t]
        trial = trial_ref[t]
        if first:
            search = None
            trial_image = image
        else:
            search_image = -STEP * image + MOMENTUM * search_image_ref[t]
            new_search_image_ref[t] = search_image
            trial_image = known_ref[t] - STEP * image
        both = jnp.concatenate([trial, trial_image], axis=0)
        basis = dot(left, both)
        new_image = dot(right, both)
        residual = dot(mixed, both)
        fresh[t] = residual
        if first:
            new_search = -STEP * residual
            new_known_ref[t] = new_image
            new_search_image_ref[t] = jnp.zeros_like(image)
        else:
            new_search = -STEP * residual + MOMENTUM * search_ref[t]
            new_known_ref[t] = new_image + MOMENTUM * search_image
        new_search_ref[t] = new_search
        new_trial_ref[t] = basis + new_search

    def own_gram(own):
        at = where_ref[0]
        mask = own_mask(where_ref)
        trial = jnp.where(mask, new_trial_ref[at], 0.0)
        known = jnp.where(mask, new_known_ref[at], 0.0)
        gram = dot(trial, trial, NT)
        projected = dot(trial, known, NT) - STEP * dot(known, fresh[at], NT)
        return gram, projected

    emit_products(
        n_row, n_col, fresh, STEP * STEP, own_gram, tiles_ref, rows_ref, cols_ref, send_row_ref, send_y_ref,
        direct, mirrored, None,
    )


def last_kernel(n_row, where_ref, recv_ref, local_ref, trial_ref, known_ref, basis_ref, rayleigh_ref, residual_ref, gq):
    gather_chunks(recv_ref, 0, gq, n_row)
    left, right, mixed, rayleigh = small_algebra(gq, n_row)
    block = local_ref[: VEC // 2, :]
    image = jnp.concatenate(unpack_pair(block, block), axis=0)
    trial = trial_ref[where_ref[0]]
    trial_image = known_ref[where_ref[0]] - STEP * image
    both = jnp.concatenate([trial, trial_image], axis=0)
    odd = where_ref[1] == 1
    basis = dot(left, both)
    residual = dot(mixed, both)
    basis_ref[...] = jnp.where(odd, swap_halves(basis), basis)[:, :HALF]
    residual_ref[...] = jnp.where(odd, swap_halves(residual), residual)[:, :HALF]
    rayleigh_ref[...] = rayleigh


def per_device(split, initial_block, matrix_tiles, tile_rows, tile_columns):
    n_x, n_zl, n_core, n_zh, n_y = split
    n_row, n_col = n_x * n_zl * n_core, n_zh * n_y
    n_tiles = n_row // 2 + n_col // 2
    half = VEC // 2
    each = half // n_row
    extra = -(-2 * each // 8) * 8
    tiles = matrix_tiles[0, 0]
    rows, cols = tile_rows[0, 0], tile_columns[0, 0]
    my_col = lax.axis_index("zh") * n_y + lax.axis_index("y")
    where = jnp.stack([my_col // 2, my_col % 2]).astype(jnp.int32)

    smem = pl.BlockSpec(memory_space=pltpu.SMEM)
    vmem = pl.BlockSpec(memory_space=pltpu.VMEM)
    f32 = jnp.float32
    state = jax.ShapeDtypeStruct((n_tiles, VEC, TILE), f32)
    send_row = jax.ShapeDtypeStruct((2, n_row // 2, half + extra, TILE), f32)
    send_y = jax.ShapeDtypeStruct((n_y, n_zh * half, TILE), f32)
    params = pltpu.CompilerParams(vmem_limit_bytes=16 * 1024 * 1024)
    partial_sums = [pltpu.VMEM((n_col // 2, VEC, TILE), f32), pltpu.VMEM((n_row // 2, VEC, TILE), f32)]

    def exchange(blocks, axes):
        return lax.all_to_all(blocks, axes, 0, 0, tiled=True)

    def spread(block, axes, count):
        return exchange(jnp.broadcast_to(block[None], (count,) + block.shape), axes)

    def reduce_row_then_y(row_blocks, y_blocks):
        mirrored = jnp.sum(exchange(row_blocks, "core"), axis=0)
        mirrored = jnp.sum(exchange(mirrored, CHIPS), axis=0)
        sums = jnp.broadcast_to(mirrored[None, half:], (n_y, extra, TILE))
        along_y = jnp.sum(exchange(jnp.concatenate([y_blocks, sums], axis=1), "y"), axis=0)
        return mirrored[:half], along_y

    def gather_row(block):
        return lax.all_gather(spread(block, CHIPS, n_row // 2), "core", axis=0)

    def apply_and_gather(row_blocks, y_blocks):
        mirrored, along_y = reduce_row_then_y(row_blocks, y_blocks)
        heard = spread(jnp.concatenate([along_y, mirrored], axis=0), "zh", n_zh)
        total = jnp.sum(heard[:, :-half], axis=0)
        blocks = total[:-extra].reshape(n_zh, half, TILE) + heard[:, -half:]
        mine = lax.dynamic_index_in_dim(blocks, lax.axis_index("zh"), 0, False)
        from_row = gather_row(jnp.concatenate([mine, total[-extra:]], axis=0))
        return from_row, spread(blocks.reshape(n_zh * half, TILE), "y", n_y)

    def apply_locally(row_blocks, y_blocks):
        mirrored, along_y = reduce_row_then_y(row_blocks, y_blocks)
        sums = jnp.broadcast_to(along_y[None, -extra:], (n_zh, extra, TILE))
        blocks = along_y[:-extra].reshape(n_zh, half, TILE)
        along_z = jnp.sum(exchange(jnp.concatenate([blocks, sums], axis=1), "zh"), axis=0)
        return along_z[:half] + mirrored, gather_row(along_z[half:])

    start = jnp.concatenate([initial_block[:half], initial_block[half:]], axis=1)
    start = jnp.concatenate([start, jnp.zeros((extra, TILE), f32)], axis=0)
    along_z = spread(start[:half], "zh", n_zh)
    from_row, from_col = gather_row(start), spread(along_z.reshape(n_zh * half, TILE), "y", n_y)
    trial, row_blocks, y_blocks = pl.pallas_call(
        functools.partial(first_kernel, n_row, n_col),
        out_shape=(state, send_row, send_y),
        in_specs=[smem] * 3 + [vmem] * 3,
        out_specs=(vmem,) * 3,
        scratch_shapes=partial_sums,
        compiler_params=params,
    )(where, rows, cols, tiles, from_row, from_col)
    carried = (trial,)
    for iteration in range(ITERS):
        from_row, from_col = apply_and_gather(row_blocks, y_blocks)
        *carried, row_blocks, y_blocks = pl.pallas_call(
            functools.partial(middle_kernel, iteration == 0, n_row, n_col),
            out_shape=(state,) * 4 + (send_row, send_y),
            in_specs=[smem] * 3 + [vmem] * (3 + len(carried)),
            out_specs=(vmem,) * 6,
            scratch_shapes=partial_sums
            + [pltpu.VMEM((n_tiles, VEC, TILE), f32), pltpu.VMEM((2, half, TILE), f32)],
            input_output_aliases={6 + k: k for k in range(len(carried))},
            compiler_params=params,
        )(where, rows, cols, tiles, from_row, from_col, *carried)
    trial, known = carried[:2]
    local, sums = apply_locally(row_blocks, y_blocks)
    small = jax.ShapeDtypeStruct((VEC, VEC), f32)
    return pl.pallas_call(
        functools.partial(last_kernel, n_row),
        out_shape=(small,) * 3,
        in_specs=[smem] + [vmem] * 4,
        out_specs=(vmem,) * 3,
        scratch_shapes=[pltpu.VMEM((2, half, TILE), f32)],
        compiler_params=params,
    )(where, sums, local, trial, known)


def solution(mesh, split=SPLIT):
    fine = Mesh(mesh.devices.reshape(split), AXES)
    in_specs = (
        P(None, AXES),
        P(ROW, COL, None, None, None),
        P(ROW, COL, None),
        P(ROW, COL, None),
    )
    out_specs = (P(None, AXES), P(), P(None, AXES))
    return jax.shard_map(
        functools.partial(per_device, split),
        mesh=fine,
        in_specs=in_specs,
        out_specs=out_specs,
        check_vma=False,
    )
```

```python
import functools

import jax
import jax.numpy as jnp
from jax import lax
from jax.experimental import pallas as pl
from jax.experimental.pallas import tpu as pltpu
from jax.sharding import Mesh
from jax.sharding import PartitionSpec as P

TILE = 128
HALF = 64
VEC = 64
GROUP = 8
ITERS = 4
STEP = 0.5
MOMENTUM = 0.4
AXES = ("x", "zl", "core", "zh", "y")
ROW = ("x", "zl", "core")
CHIPS = ("x", "zl")
COL = ("zh", "y")
SPLIT = (4, 4, 2, 4, 4)


def dot(a, b, contract=((1,), (0,))):
    return lax.dot_general(
        a,
        b,
        (contract, ((), ())),
        precision=lax.Precision.HIGHEST,
        preferred_element_type=jnp.float32,
    )


NT = ((1,), (1,))


def lanes(rows):
    return lax.broadcasted_iota(jnp.int32, (rows, TILE), 1)


def swap_halves(v):
    return pltpu.roll(v, HALF, 1)


def pack_pair(tile):
    low = lanes(VEC // 2) < HALF
    top, bottom = tile[: VEC // 2], tile[VEC // 2 :]
    even = jnp.where(low, top, swap_halves(bottom))
    odd = jnp.where(low, swap_halves(top), bottom)
    return even, odd


def unpack_pair(even, odd):
    low = lanes(VEC // 2) < HALF
    top = jnp.where(low, even, swap_halves(odd))
    bottom = jnp.where(low, swap_halves(even), odd)
    return top, bottom


def inverse_cholesky(packed):
    low = lanes(VEC // 2) < HALF
    row_id = lax.broadcasted_iota(jnp.int32, (VEC // 2, TILE), 0)
    col_id = lanes(VEC // 2)
    eye_top = jnp.where(col_id - HALF == row_id, 1.0, 0.0)
    eye_bottom = jnp.where(col_id - HALF == row_id + VEC // 2, 1.0, 0.0)
    top = jnp.where(low, packed, eye_top)
    bottom = jnp.where(low, swap_halves(packed), eye_bottom)
    count = VEC // GROUP
    groups = [half[GROUP * g : GROUP * (g + 1)] for half in (top, bottom) for g in range(count // 2)]
    sub = lax.broadcasted_iota(jnp.int32, (GROUP, TILE), 0)
    lane = lanes(GROUP)

    def wide(v):
        return jnp.broadcast_to(v, (GROUP, TILE))

    out = []
    for own in range(count):
        first = own * GROUP
        columns = {
            g: [wide(groups[g][:, first + k : first + k + 1]) for k in range(GROUP)] for g in range(own, count)
        }
        rows = [wide(groups[own][k : k + 1, :]) for k in range(GROUP)]
        corner = [
            [wide(columns[own][m][k : k + 1, :]) if m >= k else None for m in range(GROUP)] for k in range(GROUP)
        ]
        scales = []
        for k in range(GROUP):
            scale = 1.0 / corner[k][k]
            scales.append(scale)
            for l in range(k + 1, GROUP):
                factor = corner[k][l] * scale
                rows[l] = rows[l] - factor * rows[k]
                for m in range(l, GROUP):
                    corner[l][m] = corner[l][m] - factor * corner[k][m]
        for g in range(own + 1, count):
            column = columns[g]
            for k in range(GROUP):
                factor = column[k] * scales[k]
                groups[g] = groups[g] - factor * rows[k]
                for m in range(k + 1, GROUP):
                    column[m] = column[m] - factor * corner[k][m]
        block, diagonal = rows[0], corner[0][0]
        for k in range(1, GROUP):
            block = jnp.where(sub == k, rows[k], block)
            diagonal = jnp.where(sub == k, corner[k][k], diagonal)
        out.append(jnp.where(lane >= HALF, block / jnp.sqrt(diagonal), 0.0))
    return jnp.concatenate(out, axis=0)


def unpack_square(packed):
    return jnp.concatenate([packed, swap_halves(packed)], axis=0)[:, :HALF]


def small_algebra(gq_ref, size):
    gram = gq_ref[0]
    projected = unpack_square(gq_ref[1])
    right = inverse_cholesky(gram)
    left = swap_halves(right)
    inverse = left[:, :HALF]
    rayleigh = dot(dot(inverse, projected), inverse, NT)
    mixed = right - dot(rayleigh, left)
    return left, right, mixed, rayleigh


def gather_chunks(recv_ref, at, gq, count):
    each = VEC // 2 // count
    for r in range(count):
        for which in range(2):
            gq[which, r * each : (r + 1) * each, :] = recv_ref[
                r % 2, r // 2, at + which * each : at + (which + 1) * each, :
            ]


def emit_products(
    n_row, n_col, q, factor, own_gram, tiles_ref, where_ref, rows_ref, cols_ref, keep_ref, give_ref, send_y_ref,
    direct, mirrored,
):
    row_tiles, col_tiles = n_col // 2, n_row // 2
    direct[...] = jnp.zeros_like(direct)
    mirrored[...] = jnp.zeros_like(mirrored)
    cross = jnp.zeros((VEC, VEC), jnp.float32)
    for t in range(tiles_ref.shape[0]):
        i, j = rows_ref[t], cols_ref[t]
        tile = tiles_ref[t]
        row_pick = q[i]
        column_pick = q[row_tiles + j]
        product = dot(column_pick, tile, NT)
        direct[i] += product
        mirrored[j] += dot(row_pick, tile)
        cross = cross + dot(product, row_pick, NT)
    gram, projected = own_gram()
    projected = projected + factor * (cross + cross.T)
    low = lanes(VEC // 2) < HALF
    each = VEC // 2 // n_row

    def pack_square(m):
        wide = jnp.concatenate([m, m], axis=1)
        return jnp.where(low, wide[: VEC // 2], wide[VEC // 2 :])

    gram, projected = pack_square(gram), pack_square(projected)
    rest = keep_ref.shape[1] - VEC // 2 - 2 * each
    parts = (slice(0, VEC // 2), slice(VEC // 2, keep_ref.shape[1]))
    second = where_ref[2] == 1
    for b in range(col_tiles):
        even, odd = pack_pair(mirrored[b])
        sums = []
        for r in (2 * b, 2 * b + 1):
            pieces = [gram[r * each : (r + 1) * each], projected[r * each : (r + 1) * each]]
            if rest:
                pieces.append(jnp.zeros((rest, TILE), jnp.float32))
            sums.append(jnp.concatenate(pieces, axis=0))
        for part, (one, two) in zip(parts, ((even, odd), sums)):
            keep_ref[b, part, :] = jnp.where(second, two, one)
            give_ref[b, part, :] = jnp.where(second, one, two)
    n_y = send_y_ref.shape[0]
    for s in range(row_tiles):
        for c, block in zip((2 * s, 2 * s + 1), pack_pair(direct[s])):
            zh, y = c // n_y, c % n_y
            send_y_ref[y, zh * (VEC // 2) : (zh + 1) * (VEC // 2), :] = block


def unpack_gathered(recv_row_ref, recv_col_ref, n_row, n_col, out):
    n_y = recv_col_ref.shape[0]
    half = VEC // 2

    def col_block(c):
        zh, y = c // n_y, c % n_y
        return recv_col_ref[y, zh * half : (zh + 1) * half, :]

    for s in range(n_col // 2):
        top, bottom = unpack_pair(col_block(2 * s), col_block(2 * s + 1))
        out[s, :half, :] = top
        out[s, half:, :] = bottom
    for b in range(n_row // 2):
        top, bottom = unpack_pair(recv_row_ref[0, b, :half, :], recv_row_ref[1, b, :half, :])
        out[n_col // 2 + b, :half, :] = top
        out[n_col // 2 + b, half:, :] = bottom


def own_mask(where_ref):
    return (lanes(VEC) // HALF) == where_ref[1]


def first_kernel(
    n_row, n_col, where_ref, rows_ref, cols_ref, tiles_ref, recv_row_ref, recv_col_ref,
    trial_ref, keep_ref, give_ref, send_y_ref, fresh, direct, mirrored, sem,
):
    unpack_gathered(recv_row_ref, recv_col_ref, n_row, n_col, fresh)
    store = pltpu.make_async_copy(fresh, trial_ref, sem)
    store.start()

    def own_gram():
        mine = fresh[where_ref[0]]
        return dot(jnp.where(own_mask(where_ref), mine, 0.0), mine, NT), jnp.zeros((VEC, VEC), jnp.float32)

    emit_products(
        n_row, n_col, fresh, 1.0, own_gram, tiles_ref, where_ref, rows_ref, cols_ref, keep_ref, give_ref, send_y_ref,
        direct, mirrored,
    )
    store.wait()


def middle_kernel(first, n_row, n_col, *refs):
    given = 1 if first else 4
    where_ref, rows_ref, cols_ref, tiles_ref, recv_row_ref, recv_col_ref = refs[:6]
    old_refs, new_refs = refs[6 : 6 + given], refs[6 + given : 10 + given]
    keep_ref, give_ref, send_y_ref, state, fresh, direct, mirrored, gq, load_sems, store_sems = refs[10 + given :]
    n_tiles = n_col // 2 + n_row // 2
    loads = [pltpu.make_async_copy(old_refs[k], state.at[k], load_sems.at[k]) for k in range(given)]
    stores = [pltpu.make_async_copy(state.at[k], new_refs[k], store_sems.at[k]) for k in range(4)]
    for load in loads:
        load.start()
    trials, knowns, searches, search_images = (state.at[k] for k in range(4))
    gather_chunks(recv_row_ref, VEC // 2, gq, n_row)
    unpack_gathered(recv_row_ref, recv_col_ref, n_row, n_col, fresh)
    left, right, mixed, _ = small_algebra(gq, n_row)
    for load in loads:
        load.wait()
    for t in range(n_tiles):
        image = fresh[t]
        trial = trials[t]
        if first:
            search_image = jnp.zeros_like(image)
            trial_image = image
        else:
            search_image = -STEP * image + MOMENTUM * search_images[t]
            trial_image = knowns[t] - STEP * image
        both = jnp.concatenate([trial, trial_image], axis=0)
        basis = dot(left, both)
        new_image = dot(right, both)
        residual = dot(mixed, both)
        fresh[t] = residual
        search = -STEP * residual
        if not first:
            search = search + MOMENTUM * searches[t]
            new_image = new_image + MOMENTUM * search_image
        trials[t] = basis + search
        knowns[t] = new_image
        searches[t] = search
        search_images[t] = search_image
    for store in stores:
        store.start()

    def own_gram():
        at = where_ref[0]
        mask = own_mask(where_ref)
        trial = jnp.where(mask, trials[at], 0.0)
        known = jnp.where(mask, knowns[at], 0.0)
        gram = dot(trial, trial, NT)
        projected = dot(trial, known, NT) - STEP * dot(known, fresh[at], NT)
        return gram, projected

    emit_products(
        n_row, n_col, fresh, STEP * STEP, own_gram, tiles_ref, where_ref, rows_ref, cols_ref, keep_ref, give_ref,
        send_y_ref, direct, mirrored,
    )
    for store in stores:
        store.wait()


def last_kernel(n_row, where_ref, recv_ref, local_ref, trial_ref, known_ref, basis_ref, rayleigh_ref, residual_ref, gq, own, sems):
    loads = [pltpu.make_async_copy(ref.at[where_ref[0]], own.at[k], sems.at[k]) for k, ref in enumerate((trial_ref, known_ref))]
    for load in loads:
        load.start()
    gather_chunks(recv_ref, 0, gq, n_row)
    left, right, mixed, rayleigh = small_algebra(gq, n_row)
    block = local_ref[: VEC // 2, :]
    image = jnp.concatenate(unpack_pair(block, block), axis=0)
    for load in loads:
        load.wait()
    trial = own[0]
    trial_image = own[1] - STEP * image
    both = jnp.concatenate([trial, trial_image], axis=0)
    odd = where_ref[1] == 1
    basis = dot(left, both)
    residual = dot(mixed, both)
    basis_ref[...] = jnp.where(odd, swap_halves(basis), basis)[:, :HALF]
    residual_ref[...] = jnp.where(odd, swap_halves(residual), residual)[:, :HALF]
    rayleigh_ref[...] = rayleigh


def per_device(split, initial_block, matrix_tiles, tile_rows, tile_columns):
    n_x, n_zl, n_core, n_zh, n_y = split
    n_row, n_col = n_x * n_zl * n_core, n_zh * n_y
    n_tiles = n_row // 2 + n_col // 2
    half = VEC // 2
    each = half // n_row
    extra = -(-2 * each // 8) * 8
    tiles = matrix_tiles[0, 0]
    rows, cols = tile_rows[0, 0], tile_columns[0, 0]
    my_col = lax.axis_index("zh") * n_y + lax.axis_index("y")
    where = jnp.stack([my_col // 2, my_col % 2, lax.axis_index("core")]).astype(jnp.int32)

    smem = pl.BlockSpec(memory_space=pltpu.SMEM)
    vmem = pl.BlockSpec(memory_space=pltpu.VMEM)
    f32 = jnp.float32
    state = pltpu.HBM((n_tiles, VEC, TILE), f32)
    hbm = pl.BlockSpec(memory_space=pltpu.HBM)
    half_row = jax.ShapeDtypeStruct((n_row // 2, half + extra, TILE), f32)
    send_y = jax.ShapeDtypeStruct((n_y, n_zh * half, TILE), f32)
    sends = (half_row, half_row, send_y)
    params = pltpu.CompilerParams(vmem_limit_bytes=20 * 1024 * 1024)
    gathered = pltpu.VMEM((n_tiles, VEC, TILE), f32)
    partial_sums = [pltpu.VMEM((n_col // 2, VEC, TILE), f32), pltpu.VMEM((n_row // 2, VEC, TILE), f32)]
    squares = pltpu.VMEM((2, half, TILE), f32)

    def exchange(blocks, axes):
        return lax.all_to_all(blocks, axes, 0, 0, tiled=True)

    def spread(block, axes, count):
        return exchange(jnp.broadcast_to(block[None], (count,) + block.shape), axes)

    def reduce_row_and_y(keep, give, y_blocks):
        along_y = jnp.sum(exchange(y_blocks, "y"), axis=0)
        both_cores = keep + lax.ppermute(give, "core", [(0, 1), (1, 0)])
        return jnp.sum(exchange(both_cores, CHIPS), axis=0), along_y

    def gather_row(block):
        return lax.all_gather(spread(block, CHIPS, n_row // 2), "core", axis=0)

    def apply_and_gather(keep, give, y_blocks):
        mirrored, along_y = reduce_row_and_y(keep, give, y_blocks)
        heard = spread(jnp.concatenate([along_y, mirrored], axis=0), "zh", n_zh)
        n_direct = n_zh * half
        blocks = jnp.sum(heard[:, :n_direct], axis=0).reshape(n_zh, half, TILE) + heard[:, n_direct : n_direct + half]
        sums = jnp.sum(heard[:, n_direct + half :], axis=0)
        from_col = spread(jnp.concatenate([blocks.reshape(n_direct, TILE), sums], axis=0), "y", n_y)
        mine = lax.dynamic_index_in_dim(blocks, lax.axis_index("zh"), 0, False)
        sums = jnp.sum(from_col[:, n_direct:], axis=0)
        return gather_row(jnp.concatenate([mine, sums], axis=0)), from_col

    def apply_locally(keep, give, y_blocks):
        mirrored, along_y = reduce_row_and_y(keep, give, y_blocks)
        sums = jnp.broadcast_to(mirrored[None, half:], (n_zh, extra, TILE))
        blocks = along_y.reshape(n_zh, half, TILE)
        along_z = jnp.sum(exchange(jnp.concatenate([blocks, sums], axis=1), "zh"), axis=0)
        sums = jnp.sum(spread(along_z[half:], "y", n_y), axis=0)
        return along_z[:half] + mirrored[:half], gather_row(sums)

    start = jnp.concatenate([initial_block[:half], initial_block[half:]], axis=1)
    along_z = spread(start, "zh", n_zh)
    from_col = spread(along_z.reshape(n_zh * half, TILE), "y", n_y)
    from_row = gather_row(start)
    trial, *messages = pl.pallas_call(
        functools.partial(first_kernel, n_row, n_col),
        out_shape=(state,) + sends,
        in_specs=[smem] * 3 + [vmem] * 3,
        out_specs=(hbm,) + (vmem,) * 3,
        scratch_shapes=[gathered] + partial_sums + [pltpu.SemaphoreType.DMA],
        compiler_params=params,
    )(where, rows, cols, tiles, from_row, from_col)
    carried = [trial]
    for iteration in range(ITERS):
        from_row, from_col = apply_and_gather(*messages)
        results = pl.pallas_call(
            functools.partial(middle_kernel, iteration == 0, n_row, n_col),
            out_shape=(state,) * 4 + sends,
            in_specs=[smem] * 3 + [vmem] * 3 + [hbm] * len(carried),
            out_specs=(hbm,) * 4 + (vmem,) * 3,
            scratch_shapes=[pltpu.VMEM((4, n_tiles, VEC, TILE), f32), gathered]
            + partial_sums
            + [squares, pltpu.SemaphoreType.DMA((4,)), pltpu.SemaphoreType.DMA((4,))],
            input_output_aliases={6 + k: k for k in range(len(carried))},
            compiler_params=params,
        )(where, rows, cols, tiles, from_row, from_col, *[pltpu.with_memory_space_constraint(c, pltpu.HBM) for c in carried])
        carried, messages = results[:4], results[4:]
    local, sums = apply_locally(*messages)
    small = jax.ShapeDtypeStruct((VEC, VEC), f32)
    return pl.pallas_call(
        functools.partial(last_kernel, n_row),
        out_shape=(small,) * 3,
        in_specs=[smem] + [vmem] * 2 + [hbm] * 2,
        out_specs=(vmem,) * 3,
        scratch_shapes=[squares, pltpu.VMEM((2, VEC, TILE), f32), pltpu.SemaphoreType.DMA((2,))],
        compiler_params=params,
    )(where, sums, local, carried[0], carried[1])


def solution(mesh, split=SPLIT):
    fine = Mesh(mesh.devices.reshape(split), AXES)
    in_specs = (
        P(None, AXES),
        P(ROW, COL, None, None, None),
        P(ROW, COL, None),
        P(ROW, COL, None),
    )
    out_specs = (P(None, AXES), P(), P(None, AXES))
    return jax.shard_map(
        functools.partial(per_device, split),
        mesh=fine,
        in_specs=in_specs,
        out_specs=out_specs,
        check_vma=False,
    )
```

```python
import functools

import jax
import jax.numpy as jnp
from jax import lax
from jax.experimental import pallas as pl
from jax.experimental.pallas import tpu as pltpu
from jax.sharding import Mesh
from jax.sharding import PartitionSpec as P

TILE = 128
HALF = 64
VEC = 64
GROUP = 8
PIECES = 4
GIVEN = (1, 3, 4, 4)
STORED = (3, 4, 4, 0)
ITERS = 4
STEP = 0.5
MOMENTUM = 0.4
AXES = ("x", "zl", "core", "zh", "y")
ROW = ("x", "zl", "core")
CHIPS = ("x", "zl")
COL = ("zh", "y")
SPLIT = (4, 4, 2, 4, 4)


def dot(a, b, contract=((1,), (0,))):
    return lax.dot_general(
        a,
        b,
        (contract, ((), ())),
        precision=lax.Precision.HIGHEST,
        preferred_element_type=jnp.float32,
    )


NT = ((1,), (1,))


def lanes(rows):
    return lax.broadcasted_iota(jnp.int32, (rows, TILE), 1)


def swap_halves(v):
    return pltpu.roll(v, HALF, 1)


def pack_pair(tile):
    low = lanes(VEC // 2) < HALF
    top, bottom = tile[: VEC // 2], tile[VEC // 2 :]
    even = jnp.where(low, top, swap_halves(bottom))
    odd = jnp.where(low, swap_halves(top), bottom)
    return even, odd


def unpack_pair(even, odd):
    low = lanes(VEC // 2) < HALF
    top = jnp.where(low, even, swap_halves(odd))
    bottom = jnp.where(low, swap_halves(even), odd)
    return top, bottom


def inverse_cholesky(packed):
    low = lanes(VEC // 2) < HALF
    row_id = lax.broadcasted_iota(jnp.int32, (VEC // 2, TILE), 0)
    col_id = lanes(VEC // 2)
    eye_top = jnp.where(col_id - HALF == row_id, 1.0, 0.0)
    eye_bottom = jnp.where(col_id - HALF == row_id + VEC // 2, 1.0, 0.0)
    top = jnp.where(low, packed, eye_top)
    bottom = jnp.where(low, swap_halves(packed), eye_bottom)
    count = VEC // GROUP
    groups = [half[GROUP * g : GROUP * (g + 1)] for half in (top, bottom) for g in range(count // 2)]
    sub = lax.broadcasted_iota(jnp.int32, (GROUP, TILE), 0)
    lane = lanes(GROUP)

    def wide(v):
        return jnp.broadcast_to(v, (GROUP, TILE))

    out = []
    for own in range(count):
        first = own * GROUP
        columns = {
            g: [wide(groups[g][:, first + k : first + k + 1]) for k in range(GROUP)] for g in range(own, count)
        }
        rows = [wide(groups[own][k : k + 1, :]) for k in range(GROUP)]
        corner = [
            [wide(columns[own][m][k : k + 1, :]) if m >= k else None for m in range(GROUP)] for k in range(GROUP)
        ]
        scales = []
        for k in range(GROUP):
            scale = 1.0 / corner[k][k]
            scales.append(scale)
            for l in range(k + 1, GROUP):
                factor = corner[k][l] * scale
                rows[l] = rows[l] - factor * rows[k]
                for m in range(l, GROUP):
                    corner[l][m] = corner[l][m] - factor * corner[k][m]
        for g in range(own + 1, count):
            column = columns[g]
            for k in range(GROUP):
                factor = column[k] * scales[k]
                groups[g] = groups[g] - factor * rows[k]
                for m in range(k + 1, GROUP):
                    column[m] = column[m] - factor * corner[k][m]
        block, diagonal = rows[0], corner[0][0]
        for k in range(1, GROUP):
            block = jnp.where(sub == k, rows[k], block)
            diagonal = jnp.where(sub == k, corner[k][k], diagonal)
        out.append(jnp.where(lane >= HALF, block / jnp.sqrt(diagonal), 0.0))
    return jnp.concatenate(out, axis=0)


def unpack_square(packed):
    return jnp.concatenate([packed, swap_halves(packed)], axis=0)[:, :HALF]


def small_algebra(recv_ref, at, n_y):
    gram, projected = sum_squares(recv_ref, at, n_y)
    projected = unpack_square(projected)
    right = inverse_cholesky(gram)
    left = swap_halves(right)
    inverse = left[:, :HALF]
    rayleigh = dot(dot(inverse, projected), inverse, NT)
    mixed = right - dot(rayleigh, left)
    return left, right, mixed, rayleigh


def sum_squares(recv_ref, at, n_y):
    each = VEC // 2 // n_y
    sums = []
    for which in range(2):
        starts = [at + (2 * y + which) * each for y in range(n_y)]
        sums.append(jnp.concatenate([recv_ref[0, i : i + each, :] + recv_ref[1, i : i + each, :] for i in starts], axis=0))
    return sums


def emit_products(
    n_row, n_col, q, factor, own_gram, tiles_ref, where_ref, rows_ref, cols_ref, keep_ref, give_ref, send_y_ref,
    direct, mirrored,
):
    row_tiles, col_tiles = n_col // 2, n_row // 2
    direct[...] = jnp.zeros_like(direct)
    mirrored[...] = jnp.zeros_like(mirrored)
    cross = jnp.zeros((VEC, VEC), jnp.float32)
    for t in range(tiles_ref.shape[0]):
        i, j = rows_ref[t], cols_ref[t]
        tile = tiles_ref[t]
        row_pick = q[i]
        column_pick = q[row_tiles + j]
        product = dot(column_pick, tile, NT)
        direct[i] += product
        mirrored[j] += dot(row_pick, tile)
        cross = cross + dot(product, row_pick, NT)
    gram, projected = own_gram()
    projected = projected + factor * (cross + cross.T)
    low = lanes(VEC // 2) < HALF

    def pack_square(m):
        wide = jnp.concatenate([m, m], axis=1)
        return jnp.where(low, wide[: VEC // 2], wide[VEC // 2 :])

    n_y = send_y_ref.shape[0]
    each = VEC // 2 // n_y
    at = send_y_ref.shape[1] - 2 * each
    for which, square in enumerate((pack_square(gram), pack_square(projected))):
        for y in range(n_y):
            start = at + which * each
            send_y_ref[y, start : start + each, :] = square[y * each : (y + 1) * each]
    second = where_ref[2] == 1
    for b in range(col_tiles):
        even, odd = pack_pair(mirrored[b])
        keep_ref[b] = jnp.where(second, odd, even)
        give_ref[b] = jnp.where(second, even, odd)
    for s in range(row_tiles):
        for c, block in zip((2 * s, 2 * s + 1), pack_pair(direct[s])):
            zh, y = c // n_y, c % n_y
            send_y_ref[y, zh * (VEC // 2) : (zh + 1) * (VEC // 2), :] = block


def unpack_gathered(recv_row_ref, recv_col_ref, n_row, n_col, out):
    n_y = recv_col_ref.shape[0]
    half = VEC // 2

    def col_block(c):
        zh, y = c // n_y, c % n_y
        return recv_col_ref[y, zh * half : (zh + 1) * half, :]

    for s in range(n_col // 2):
        top, bottom = unpack_pair(col_block(2 * s), col_block(2 * s + 1))
        out[s, :half, :] = top
        out[s, half:, :] = bottom
    for b in range(n_row // 2):
        top, bottom = unpack_pair(*(recv_row_ref[core, b * half : (b + 1) * half, :] for core in range(2)))
        out[n_col // 2 + b, :half, :] = top
        out[n_col // 2 + b, half:, :] = bottom


def own_mask(where_ref):
    return (lanes(VEC) // HALF) == where_ref[1]


def first_kernel(
    n_row, n_col, where_ref, rows_ref, cols_ref, tiles_ref, recv_row_ref, recv_col_ref,
    trial_ref, keep_ref, give_ref, send_y_ref, fresh, direct, mirrored, sem,
):
    unpack_gathered(recv_row_ref, recv_col_ref, n_row, n_col, fresh)
    store = pltpu.make_async_copy(fresh, trial_ref, sem)
    store.start()

    def own_gram():
        mine = fresh[where_ref[0]]
        return dot(jnp.where(own_mask(where_ref), mine, 0.0), mine, NT), jnp.zeros((VEC, VEC), jnp.float32)

    emit_products(
        n_row, n_col, fresh, 1.0, own_gram, tiles_ref, where_ref, rows_ref, cols_ref, keep_ref, give_ref, send_y_ref,
        direct, mirrored,
    )
    store.wait()


def middle_kernel(step, n_row, n_col, *refs):
    first, last = step == 0, step == ITERS - 1
    given, stored = GIVEN[step], STORED[step]
    where_ref, rows_ref, cols_ref, tiles_ref, recv_row_ref, recv_col_ref = refs[:6]
    old_refs, refs = refs[6 : 6 + given], refs[6 + given :]
    new_refs, refs = refs[: stored or 2], refs[stored or 2 :]
    keep_ref, give_ref, send_y_ref, state, fresh, direct, mirrored, load_sems, store_sems = refs
    n_tiles = n_col // 2 + n_row // 2
    piece = n_tiles // PIECES

    def moves(outside, sems, count, inward):
        result = []
        for p in range(PIECES):
            tiles = pl.ds(p * piece, piece)
            pairs = [(outside[k].at[tiles], state.at[k, tiles]) for k in range(count)]
            result.append(
                [
                    pltpu.make_async_copy(*(pair if inward else pair[::-1]), sems.at[k, p])
                    for k, pair in enumerate(pairs)
                ]
            )
        return result

    loads = moves(old_refs, load_sems, given, True)
    stores = moves(new_refs, store_sems, stored, False)
    for part in loads:
        for load in part:
            load.start()
    trials, knowns, searches, search_images = (state.at[k] for k in range(4))
    unpack_gathered(recv_row_ref, recv_col_ref, n_row, n_col, fresh)
    left, right, mixed, _ = small_algebra(recv_row_ref, n_row // 2 * (VEC // 2), recv_col_ref.shape[0])
    for t in range(n_tiles):
        if t % piece == 0:
            for load in loads[t // piece]:
                load.wait()
        image = fresh[t]
        trial = trials[t]
        trial_image = image if first else knowns[t] - STEP * image
        both = jnp.concatenate([trial, trial_image], axis=0)
        basis = dot(left, both)
        new_image = dot(right, both)
        residual = dot(mixed, both)
        fresh[t] = residual
        search = -STEP * residual
        if not first:
            search = search + MOMENTUM * searches[t]
            search_image = -STEP * image
            if given == 4:
                search_image = search_image + MOMENTUM * search_images[t]
            new_image = new_image + MOMENTUM * search_image
            if stored == 4:
                search_images[t] = search_image
        trials[t] = basis + search
        knowns[t] = new_image
        if not last:
            searches[t] = search
        if t % piece == piece - 1:
            for store in stores[t // piece]:
                store.start()
    if last:
        new_refs[0][...] = trials[where_ref[0]]
        new_refs[1][...] = knowns[where_ref[0]]

    def own_gram():
        at = where_ref[0]
        mask = own_mask(where_ref)
        trial = jnp.where(mask, trials[at], 0.0)
        known = jnp.where(mask, knowns[at], 0.0)
        gram = dot(trial, trial, NT)
        projected = dot(trial, known, NT) - STEP * dot(known, fresh[at], NT)
        return gram, projected

    emit_products(
        n_row, n_col, fresh, STEP * STEP, own_gram, tiles_ref, where_ref, rows_ref, cols_ref, keep_ref, give_ref,
        send_y_ref, direct, mirrored,
    )
    for part in stores:
        for store in part:
            store.wait()


def last_kernel(n_y, where_ref, recv_ref, local_ref, trial_ref, known_ref, basis_ref, rayleigh_ref, residual_ref):
    left, right, mixed, rayleigh = small_algebra(recv_ref, 0, n_y)
    block = local_ref[...]
    image = jnp.concatenate(unpack_pair(block, block), axis=0)
    trial = trial_ref[...]
    trial_image = known_ref[...] - STEP * image
    both = jnp.concatenate([trial, trial_image], axis=0)
    odd = where_ref[1] == 1
    basis = dot(left, both)
    residual = dot(mixed, both)
    basis_ref[...] = jnp.where(odd, swap_halves(basis), basis)[:, :HALF]
    residual_ref[...] = jnp.where(odd, swap_halves(residual), residual)[:, :HALF]
    rayleigh_ref[...] = rayleigh


def per_device(split, initial_block, matrix_tiles, tile_rows, tile_columns):
    n_x, n_zl, n_core, n_zh, n_y = split
    n_row, n_col = n_x * n_zl * n_core, n_zh * n_y
    n_tiles = n_row // 2 + n_col // 2
    half = VEC // 2
    sums_rows = 2 * (half // n_y)
    n_direct = n_zh * half
    tiles = matrix_tiles[0, 0]
    rows, cols = tile_rows[0, 0], tile_columns[0, 0]
    my_col = lax.axis_index("zh") * n_y + lax.axis_index("y")
    where = jnp.stack([my_col // 2, my_col % 2, lax.axis_index("core")]).astype(jnp.int32)

    smem = pl.BlockSpec(memory_space=pltpu.SMEM)
    vmem = pl.BlockSpec(memory_space=pltpu.VMEM)
    f32 = jnp.float32
    state = pltpu.HBM((n_tiles, VEC, TILE), f32)
    hbm = pl.BlockSpec(memory_space=pltpu.HBM)
    half_row = jax.ShapeDtypeStruct((n_row // 2, half, TILE), f32)
    send_y = jax.ShapeDtypeStruct((n_y, n_direct + sums_rows, TILE), f32)
    sends = (half_row, half_row, send_y)
    params = pltpu.CompilerParams(vmem_limit_bytes=20 * 1024 * 1024)
    gathered = pltpu.VMEM((n_tiles, VEC, TILE), f32)
    partial_sums = [pltpu.VMEM((n_col // 2, VEC, TILE), f32), pltpu.VMEM((n_row // 2, VEC, TILE), f32)]
    own_tile = jax.ShapeDtypeStruct((VEC, TILE), f32)

    def exchange(blocks, axes):
        return lax.all_to_all(blocks, axes, 0, 0, tiled=True)

    def spread(block, axes, count):
        return exchange(jnp.broadcast_to(block[None], (count,) + block.shape), axes)

    def reduce_row_and_y(keep, give, y_blocks):
        along_y = jnp.sum(exchange(y_blocks, "y"), axis=0)
        both_cores = keep + lax.ppermute(give, "core", [(0, 1), (1, 0)])
        sums = jnp.broadcast_to(along_y[None, n_direct:], (n_row // 2, sums_rows, TILE))
        mirrored = jnp.sum(exchange(jnp.concatenate([both_cores, sums], axis=1), CHIPS), axis=0)
        return mirrored, along_y[:n_direct]

    def gather_chips(block):
        return spread(block, CHIPS, n_row // 2).reshape(n_row // 2 * half, TILE)

    def apply_and_gather(keep, give, y_blocks):
        mirrored, along_y = reduce_row_and_y(keep, give, y_blocks)
        heard = spread(jnp.concatenate([along_y, mirrored], axis=0), "zh", n_zh)
        blocks = jnp.sum(heard[:, :n_direct], axis=0).reshape(n_zh, half, TILE) + heard[:, n_direct : n_direct + half]
        sums = jnp.sum(heard[:, n_direct + half :], axis=0)
        mine = lax.dynamic_index_in_dim(blocks, lax.axis_index("zh"), 0, False)
        from_chips = gather_chips(mine)
        from_col = lax.all_gather(jnp.concatenate([blocks.reshape(n_direct, TILE), sums], axis=0), "y", axis=0)
        sums = from_col[:, n_direct:].reshape(n_y * sums_rows, TILE)
        return lax.all_gather(jnp.concatenate([from_chips, sums], axis=0), "core", axis=0), from_col

    def apply_locally(keep, give, y_blocks):
        mirrored, along_y = reduce_row_and_y(keep, give, y_blocks)
        sums = jnp.broadcast_to(mirrored[None, half:], (n_zh, sums_rows, TILE))
        blocks = along_y.reshape(n_zh, half, TILE)
        along_z = jnp.sum(exchange(jnp.concatenate([blocks, sums], axis=1), "zh"), axis=0)
        sums = spread(along_z[half:], "y", n_y).reshape(n_y * sums_rows, TILE)
        return along_z[:half] + mirrored[:half], lax.all_gather(sums, "core", axis=0)

    start = jnp.concatenate([initial_block[:half], initial_block[half:]], axis=1)
    along_z = spread(start, "zh", n_zh)
    from_chips = gather_chips(start)
    from_col = lax.all_gather(along_z.reshape(n_direct, TILE), "y", axis=0)
    from_row = lax.all_gather(from_chips, "core", axis=0)
    trial, *messages = pl.pallas_call(
        functools.partial(first_kernel, n_row, n_col),
        out_shape=(state,) + sends,
        in_specs=[smem] * 3 + [vmem] * 3,
        out_specs=(hbm,) + (vmem,) * 3,
        scratch_shapes=[gathered] + partial_sums + [pltpu.SemaphoreType.DMA],
        compiler_params=params,
    )(where, rows, cols, tiles, from_row, from_col)
    carried = [trial]
    for step in range(ITERS):
        from_row, from_col = apply_and_gather(*messages)
        stored = STORED[step]
        kept = stored or 2
        carried = [pltpu.with_memory_space_constraint(array, pltpu.HBM) for array in carried]
        results = pl.pallas_call(
            functools.partial(middle_kernel, step, n_row, n_col),
            out_shape=((state,) * stored or (own_tile,) * 2) + sends,
            in_specs=[smem] * 3 + [vmem] * 3 + [hbm] * len(carried),
            out_specs=((hbm,) * stored or (vmem,) * 2) + (vmem,) * 3,
            scratch_shapes=[pltpu.VMEM((4, n_tiles, VEC, TILE), f32), gathered]
            + partial_sums
            + [pltpu.SemaphoreType.DMA((4, PIECES)), pltpu.SemaphoreType.DMA((4, PIECES))],
            input_output_aliases={6 + k: k for k in range(min(len(carried), stored))},
            compiler_params=params,
        )(where, rows, cols, tiles, from_row, from_col, *carried)
        carried, messages = results[:kept], results[kept:]
    local, sums = apply_locally(*messages)
    small = jax.ShapeDtypeStruct((VEC, VEC), f32)
    return pl.pallas_call(
        functools.partial(last_kernel, n_y),
        out_shape=(small,) * 3,
        in_specs=[smem] + [vmem] * 4,
        out_specs=(vmem,) * 3,
        compiler_params=params,
    )(where, sums, local, *carried)


def solution(mesh, split=SPLIT):
    fine = Mesh(mesh.devices.reshape(split), AXES)
    in_specs = (
        P(None, AXES),
        P(ROW, COL, None, None, None),
        P(ROW, COL, None),
        P(ROW, COL, None),
    )
    out_specs = (P(None, AXES), P(), P(None, AXES))
    return jax.shard_map(
        functools.partial(per_device, split),
        mesh=fine,
        in_specs=in_specs,
        out_specs=out_specs,
        check_vma=False,
    )
```

```python
import functools

import jax
import jax.numpy as jnp
from jax import lax
from jax.experimental import pallas as pl
from jax.experimental.pallas import tpu as pltpu
from jax.sharding import Mesh
from jax.sharding import PartitionSpec as P

TILE = 128
HALF = 64
VEC = 64
GROUP = 8
PIECES = 4
GIVEN = (1, 3, 4, 4)
STORED = (3, 4, 4, 0)
ITERS = 4
STEP = 0.5
MOMENTUM = 0.4
AXES = ("x", "zl", "core", "zh", "y")
ROW = ("x", "zl", "core")
CHIPS = ("x", "zl")
COL = ("zh", "y")
SPLIT = (4, 4, 2, 4, 4)


def dot(a, b, contract=((1,), (0,))):
    return lax.dot_general(
        a,
        b,
        (contract, ((), ())),
        precision=lax.Precision.HIGHEST,
        preferred_element_type=jnp.float32,
    )


NT = ((1,), (1,))


def lanes(rows):
    return lax.broadcasted_iota(jnp.int32, (rows, TILE), 1)


def swap_halves(v):
    return pltpu.roll(v, HALF, 1)


def pack_pair(tile):
    low = lanes(VEC // 2) < HALF
    top, bottom = tile[: VEC // 2], tile[VEC // 2 :]
    even = jnp.where(low, top, swap_halves(bottom))
    odd = jnp.where(low, swap_halves(top), bottom)
    return even, odd


def unpack_pair(even, odd):
    low = lanes(VEC // 2) < HALF
    top = jnp.where(low, even, swap_halves(odd))
    bottom = jnp.where(low, swap_halves(even), odd)
    return top, bottom


def inverse_cholesky(packed):
    low = lanes(VEC // 2) < HALF
    row_id = lax.broadcasted_iota(jnp.int32, (VEC // 2, TILE), 0)
    col_id = lanes(VEC // 2)
    eye_top = jnp.where(col_id - HALF == row_id, 1.0, 0.0)
    eye_bottom = jnp.where(col_id - HALF == row_id + VEC // 2, 1.0, 0.0)
    top = jnp.where(low, packed, eye_top)
    bottom = jnp.where(low, swap_halves(packed), eye_bottom)
    count = VEC // GROUP
    groups = [half[GROUP * g : GROUP * (g + 1)] for half in (top, bottom) for g in range(count // 2)]
    sub = lax.broadcasted_iota(jnp.int32, (GROUP, TILE), 0)
    lane = lanes(GROUP)

    def wide(v):
        return jnp.broadcast_to(v, (GROUP, TILE))

    out = []
    for own in range(count):
        first = own * GROUP
        columns = {
            g: [wide(groups[g][:, first + k : first + k + 1]) for k in range(GROUP)] for g in range(own, count)
        }
        rows = [wide(groups[own][k : k + 1, :]) for k in range(GROUP)]
        corner = [
            [wide(columns[own][m][k : k + 1, :]) if m >= k else None for m in range(GROUP)] for k in range(GROUP)
        ]
        scales = []
        for k in range(GROUP):
            scale = 1.0 / corner[k][k]
            scales.append(scale)
            for l in range(k + 1, GROUP):
                factor = corner[k][l] * scale
                rows[l] = rows[l] - factor * rows[k]
                for m in range(l, GROUP):
                    corner[l][m] = corner[l][m] - factor * corner[k][m]
        for g in range(own + 1, count):
            column = columns[g]
            for k in range(GROUP):
                factor = column[k] * scales[k]
                groups[g] = groups[g] - factor * rows[k]
                for m in range(k + 1, GROUP):
                    column[m] = column[m] - factor * corner[k][m]
        block, diagonal = rows[0], corner[0][0]
        for k in range(1, GROUP):
            block = jnp.where(sub == k, rows[k], block)
            diagonal = jnp.where(sub == k, corner[k][k], diagonal)
        out.append(jnp.where(lane >= HALF, block / jnp.sqrt(diagonal), 0.0))
    return jnp.concatenate(out, axis=0)


def unpack_square(packed):
    return jnp.concatenate([packed, swap_halves(packed)], axis=0)[:, :HALF]


def small_algebra(recv_ref, at, n_y):
    gram, projected = sum_squares(recv_ref, at, n_y)
    projected = unpack_square(projected)
    right = inverse_cholesky(gram)
    left = swap_halves(right)
    inverse = left[:, :HALF]
    rayleigh = dot(dot(inverse, projected), inverse, NT)
    mixed = right - dot(rayleigh, left)
    return left, right, mixed, rayleigh


def sum_squares(recv_ref, at, n_y):
    each = VEC // 2 // n_y
    sums = []
    for which in range(2):
        starts = [at + (2 * y + which) * each for y in range(n_y)]
        sums.append(jnp.concatenate([recv_ref[0, i : i + each, :] + recv_ref[1, i : i + each, :] for i in starts], axis=0))
    return sums


def emit_products(
    n_row, n_col, q, factor, own_gram, tiles_ref, where_ref, rows_ref, cols_ref, keep_ref, give_ref, send_y_ref,
    direct, mirrored,
):
    row_tiles, col_tiles = n_col // 2, n_row // 2
    direct[...] = jnp.zeros_like(direct)
    mirrored[...] = jnp.zeros_like(mirrored)
    cross = jnp.zeros((VEC, VEC), jnp.float32)
    for t in range(tiles_ref.shape[0]):
        i, j = rows_ref[t], cols_ref[t]
        tile = tiles_ref[t]
        row_pick = q[i]
        column_pick = q[row_tiles + j]
        product = dot(column_pick, tile, NT)
        direct[i] += product
        mirrored[j] += dot(row_pick, tile)
        cross = cross + dot(product, row_pick, NT)
    gram, projected = own_gram()
    projected = projected + factor * (cross + cross.T)
    low = lanes(VEC // 2) < HALF

    def pack_square(m):
        wide = jnp.concatenate([m, m], axis=1)
        return jnp.where(low, wide[: VEC // 2], wide[VEC // 2 :])

    n_y = send_y_ref.shape[0]
    each = VEC // 2 // n_y
    at = send_y_ref.shape[1] - 2 * each
    for which, square in enumerate((pack_square(gram), pack_square(projected))):
        for y in range(n_y):
            start = at + which * each
            send_y_ref[y, start : start + each, :] = square[y * each : (y + 1) * each]
    second = where_ref[2] == 1
    for b in range(col_tiles):
        even, odd = pack_pair(mirrored[b])
        keep_ref[b] = jnp.where(second, odd, even)
        give_ref[b] = jnp.where(second, even, odd)
    for s in range(row_tiles):
        for c, block in zip((2 * s, 2 * s + 1), pack_pair(direct[s])):
            zh, y = c // n_y, c % n_y
            send_y_ref[y, zh * (VEC // 2) : (zh + 1) * (VEC // 2), :] = block


def unpack_gathered(recv_row_ref, recv_col_ref, n_row, n_col, out):
    n_y = recv_col_ref.shape[0]
    half = VEC // 2

    def col_block(c):
        zh, y = c // n_y, c % n_y
        return recv_col_ref[y, zh * half : (zh + 1) * half, :]

    for s in range(n_col // 2):
        top, bottom = unpack_pair(col_block(2 * s), col_block(2 * s + 1))
        out[s, :half, :] = top
        out[s, half:, :] = bottom
    for b in range(n_row // 2):
        top, bottom = unpack_pair(*(recv_row_ref[core, b * half : (b + 1) * half, :] for core in range(2)))
        out[n_col // 2 + b, :half, :] = top
        out[n_col // 2 + b, half:, :] = bottom


def own_mask(where_ref):
    return (lanes(VEC) // HALF) == where_ref[1]


def first_kernel(
    n_row, n_col, where_ref, rows_ref, cols_ref, tiles_ref, recv_row_ref, recv_col_ref,
    trial_ref, keep_ref, give_ref, send_y_ref, fresh, direct, mirrored, sem,
):
    unpack_gathered(recv_row_ref, recv_col_ref, n_row, n_col, fresh)
    store = pltpu.make_async_copy(fresh, trial_ref, sem)
    store.start()

    def own_gram():
        mine = fresh[where_ref[0]]
        return dot(jnp.where(own_mask(where_ref), mine, 0.0), mine, NT), jnp.zeros((VEC, VEC), jnp.float32)

    emit_products(
        n_row, n_col, fresh, 1.0, own_gram, tiles_ref, where_ref, rows_ref, cols_ref, keep_ref, give_ref, send_y_ref,
        direct, mirrored,
    )
    store.wait()


def middle_kernel(step, n_row, n_col, *refs):
    first, last = step == 0, step == ITERS - 1
    given, stored = GIVEN[step], STORED[step]
    where_ref, rows_ref, cols_ref, tiles_ref, recv_row_ref, recv_col_ref = refs[:6]
    old_refs, refs = refs[6 : 6 + given], refs[6 + given :]
    new_refs, refs = refs[: stored or 2], refs[stored or 2 :]
    keep_ref, give_ref, send_y_ref, state, fresh, direct, mirrored, load_sems, store_sems = refs
    n_tiles = n_col // 2 + n_row // 2
    piece = n_tiles // PIECES

    def moves(outside, sems, count, inward):
        result = []
        for p in range(PIECES):
            tiles = pl.ds(p * piece, piece)
            pairs = [(outside[k].at[tiles], state.at[k, tiles]) for k in range(count)]
            result.append(
                [
                    pltpu.make_async_copy(*(pair if inward else pair[::-1]), sems.at[k, p])
                    for k, pair in enumerate(pairs)
                ]
            )
        return result

    loads = moves(old_refs, load_sems, given, True)
    stores = moves(new_refs, store_sems, stored, False)
    for part in loads:
        for load in part:
            load.start()
    trials, knowns, searches, search_images = (state.at[k] for k in range(4))
    unpack_gathered(recv_row_ref, recv_col_ref, n_row, n_col, fresh)
    left, right, mixed, _ = small_algebra(recv_row_ref, n_row // 2 * (VEC // 2), recv_col_ref.shape[0])
    coefficients = jnp.concatenate([left, right, mixed], axis=0)
    for t in range(n_tiles):
        if t % piece == 0:
            for load in loads[t // piece]:
                load.wait()
        image = fresh[t]
        trial = trials[t]
        trial_image = image if first else knowns[t] - STEP * image
        both = jnp.concatenate([trial, trial_image], axis=0)
        mixtures = dot(coefficients, both)
        basis, new_image, residual = (mixtures[VEC * k : VEC * (k + 1)] for k in range(3))
        fresh[t] = residual
        search = -STEP * residual
        if not first:
            search = search + MOMENTUM * searches[t]
            search_image = -STEP * image
            if given == 4:
                search_image = search_image + MOMENTUM * search_images[t]
            new_image = new_image + MOMENTUM * search_image
            if stored == 4:
                search_images[t] = search_image
        trials[t] = basis + search
        knowns[t] = new_image
        if not last:
            searches[t] = search
        if t % piece == piece - 1:
            for store in stores[t // piece]:
                store.start()
    if last:
        new_refs[0][...] = trials[where_ref[0]]
        new_refs[1][...] = knowns[where_ref[0]]

    def own_gram():
        at = where_ref[0]
        mask = own_mask(where_ref)
        trial = jnp.where(mask, trials[at], 0.0)
        known = jnp.where(mask, knowns[at], 0.0)
        gram = dot(trial, trial, NT)
        projected = dot(trial, known, NT) - STEP * dot(known, fresh[at], NT)
        return gram, projected

    emit_products(
        n_row, n_col, fresh, STEP * STEP, own_gram, tiles_ref, where_ref, rows_ref, cols_ref, keep_ref, give_ref,
        send_y_ref, direct, mirrored,
    )
    for part in stores:
        for store in part:
            store.wait()


def last_kernel(n_y, where_ref, recv_ref, local_ref, trial_ref, known_ref, basis_ref, rayleigh_ref, residual_ref):
    left, right, mixed, rayleigh = small_algebra(recv_ref, 0, n_y)
    block = local_ref[...]
    image = jnp.concatenate(unpack_pair(block, block), axis=0)
    trial = trial_ref[...]
    trial_image = known_ref[...] - STEP * image
    both = jnp.concatenate([trial, trial_image], axis=0)
    odd = where_ref[1] == 1
    basis = dot(left, both)
    residual = dot(mixed, both)
    basis_ref[...] = jnp.where(odd, swap_halves(basis), basis)[:, :HALF]
    residual_ref[...] = jnp.where(odd, swap_halves(residual), residual)[:, :HALF]
    rayleigh_ref[...] = rayleigh


def per_device(split, initial_block, matrix_tiles, tile_rows, tile_columns):
    n_x, n_zl, n_core, n_zh, n_y = split
    n_row, n_col = n_x * n_zl * n_core, n_zh * n_y
    n_tiles = n_row // 2 + n_col // 2
    half = VEC // 2
    sums_rows = 2 * (half // n_y)
    n_direct = n_zh * half
    tiles = matrix_tiles[0, 0]
    rows, cols = tile_rows[0, 0], tile_columns[0, 0]
    my_col = lax.axis_index("zh") * n_y + lax.axis_index("y")
    where = jnp.stack([my_col // 2, my_col % 2, lax.axis_index("core")]).astype(jnp.int32)

    smem = pl.BlockSpec(memory_space=pltpu.SMEM)
    vmem = pl.BlockSpec(memory_space=pltpu.VMEM)
    f32 = jnp.float32
    state = pltpu.HBM((n_tiles, VEC, TILE), f32)
    hbm = pl.BlockSpec(memory_space=pltpu.HBM)
    half_row = jax.ShapeDtypeStruct((n_row // 2, half, TILE), f32)
    send_y = jax.ShapeDtypeStruct((n_y, n_direct + sums_rows, TILE), f32)
    sends = (half_row, half_row, send_y)
    params = pltpu.CompilerParams(vmem_limit_bytes=20 * 1024 * 1024)
    gathered = pltpu.VMEM((n_tiles, VEC, TILE), f32)
    partial_sums = [pltpu.VMEM((n_col // 2, VEC, TILE), f32), pltpu.VMEM((n_row // 2, VEC, TILE), f32)]
    own_tile = jax.ShapeDtypeStruct((VEC, TILE), f32)

    def exchange(blocks, axes):
        return lax.all_to_all(blocks, axes, 0, 0, tiled=True)

    def spread(block, axes, count):
        return exchange(jnp.broadcast_to(block[None], (count,) + block.shape), axes)

    def reduce_row_and_y(keep, give, y_blocks):
        both_cores = keep + lax.ppermute(give, "core", [(0, 1), (1, 0)])
        from_y, both_cores = lax.optimization_barrier((exchange(y_blocks, "y"), both_cores))
        along_y = jnp.sum(from_y, axis=0)
        sums = jnp.broadcast_to(along_y[None, n_direct:], (n_row // 2, sums_rows, TILE))
        mirrored = jnp.sum(exchange(jnp.concatenate([both_cores, sums], axis=1), CHIPS), axis=0)
        return mirrored, along_y[:n_direct]

    def gather_chips(block):
        return spread(block, CHIPS, n_row // 2).reshape(n_row // 2 * half, TILE)

    def apply_and_gather(keep, give, y_blocks):
        mirrored, along_y = reduce_row_and_y(keep, give, y_blocks)
        heard = spread(jnp.concatenate([along_y, mirrored], axis=0), "zh", n_zh)
        blocks = jnp.sum(heard[:, :n_direct], axis=0).reshape(n_zh, half, TILE) + heard[:, n_direct : n_direct + half]
        sums = jnp.sum(heard[:, n_direct + half :], axis=0)
        mine = lax.dynamic_index_in_dim(blocks, lax.axis_index("zh"), 0, False)
        from_chips = gather_chips(mine)
        from_col = lax.all_gather(jnp.concatenate([blocks.reshape(n_direct, TILE), sums], axis=0), "y", axis=0)
        sums = from_col[:, n_direct:].reshape(n_y * sums_rows, TILE)
        return lax.all_gather(jnp.concatenate([from_chips, sums], axis=0), "core", axis=0), from_col

    def apply_locally(keep, give, y_blocks):
        mirrored, along_y = reduce_row_and_y(keep, give, y_blocks)
        sums = jnp.broadcast_to(mirrored[None, half:], (n_zh, sums_rows, TILE))
        blocks = along_y.reshape(n_zh, half, TILE)
        along_z = jnp.sum(exchange(jnp.concatenate([blocks, sums], axis=1), "zh"), axis=0)
        sums = spread(along_z[half:], "y", n_y).reshape(n_y * sums_rows, TILE)
        return along_z[:half] + mirrored[:half], lax.all_gather(sums, "core", axis=0)

    start = jnp.concatenate([initial_block[:half], initial_block[half:]], axis=1)
    along_z = spread(start, "zh", n_zh)
    from_chips = gather_chips(start)
    from_col = lax.all_gather(along_z.reshape(n_direct, TILE), "y", axis=0)
    from_row = lax.all_gather(from_chips, "core", axis=0)
    trial, *messages = pl.pallas_call(
        functools.partial(first_kernel, n_row, n_col),
        out_shape=(state,) + sends,
        in_specs=[smem] * 3 + [vmem] * 3,
        out_specs=(hbm,) + (vmem,) * 3,
        scratch_shapes=[gathered] + partial_sums + [pltpu.SemaphoreType.DMA],
        compiler_params=params,
    )(where, rows, cols, tiles, from_row, from_col)
    carried = [trial]
    for step in range(ITERS):
        from_row, from_col = apply_and_gather(*messages)
        stored = STORED[step]
        kept = stored or 2
        carried = [pltpu.with_memory_space_constraint(array, pltpu.HBM) for array in carried]
        results = pl.pallas_call(
            functools.partial(middle_kernel, step, n_row, n_col),
            out_shape=((state,) * stored or (own_tile,) * 2) + sends,
            in_specs=[smem] * 3 + [vmem] * 3 + [hbm] * len(carried),
            out_specs=((hbm,) * stored or (vmem,) * 2) + (vmem,) * 3,
            scratch_shapes=[pltpu.VMEM((4, n_tiles, VEC, TILE), f32), gathered]
            + partial_sums
            + [pltpu.SemaphoreType.DMA((4, PIECES)), pltpu.SemaphoreType.DMA((4, PIECES))],
            input_output_aliases={6 + k: k for k in range(min(len(carried), stored))},
            compiler_params=params,
        )(where, rows, cols, tiles, from_row, from_col, *carried)
        carried, messages = results[:kept], results[kept:]
    local, sums = apply_locally(*messages)
    small = jax.ShapeDtypeStruct((VEC, VEC), f32)
    return pl.pallas_call(
        functools.partial(last_kernel, n_y),
        out_shape=(small,) * 3,
        in_specs=[smem] + [vmem] * 4,
        out_specs=(vmem,) * 3,
        compiler_params=params,
    )(where, sums, local, *carried)


def solution(mesh, split=SPLIT):
    fine = Mesh(mesh.devices.reshape(split), AXES)
    in_specs = (
        P(None, AXES),
        P(ROW, COL, None, None, None),
        P(ROW, COL, None),
        P(ROW, COL, None),
    )
    out_specs = (P(None, AXES), P(), P(None, AXES))
    return jax.shard_map(
        functools.partial(per_device, split),
        mesh=fine,
        in_specs=in_specs,
        out_specs=out_specs,
        check_vma=False,
    )
```

```python
import functools

import jax
import jax.numpy as jnp
from jax import lax
from jax.experimental import pallas as pl
from jax.experimental.pallas import tpu as pltpu
from jax.sharding import Mesh
from jax.sharding import PartitionSpec as P

TILE = 128
HALF = 64
VEC = 64
GROUP = 8
PIECES = 4
GIVEN = (1, 3, 4, 4)
STORED = (3, 4, 4, 0)
ITERS = 4
STEP = 0.5
MOMENTUM = 0.4
AXES = ("x", "zl", "core", "zh", "y")
ROW = ("x", "zl", "core")
CHIPS = ("x", "zl")
COL = ("zh", "y")
SPLIT = (4, 4, 2, 4, 4)


def dot(a, b, contract=((1,), (0,))):
    return lax.dot_general(
        a,
        b,
        (contract, ((), ())),
        precision=lax.Precision.HIGHEST,
        preferred_element_type=jnp.float32,
    )


NT = ((1,), (1,))


def lanes(rows):
    return lax.broadcasted_iota(jnp.int32, (rows, TILE), 1)


def swap_halves(v):
    return pltpu.roll(v, HALF, 1)


def pack_pair(tile):
    low = lanes(VEC // 2) < HALF
    top, bottom = tile[: VEC // 2], tile[VEC // 2 :]
    even = jnp.where(low, top, swap_halves(bottom))
    odd = jnp.where(low, swap_halves(top), bottom)
    return even, odd


def unpack_pair(even, odd):
    low = lanes(VEC // 2) < HALF
    top = jnp.where(low, even, swap_halves(odd))
    bottom = jnp.where(low, swap_halves(even), odd)
    return top, bottom


def inverse_cholesky(packed):
    low = lanes(VEC // 2) < HALF
    row_id = lax.broadcasted_iota(jnp.int32, (VEC // 2, TILE), 0)
    col_id = lanes(VEC // 2)
    eye_top = jnp.where(col_id - HALF == row_id, 1.0, 0.0)
    eye_bottom = jnp.where(col_id - HALF == row_id + VEC // 2, 1.0, 0.0)
    top = jnp.where(low, packed, eye_top)
    bottom = jnp.where(low, swap_halves(packed), eye_bottom)
    count = VEC // GROUP
    groups = [half[GROUP * g : GROUP * (g + 1)] for half in (top, bottom) for g in range(count // 2)]
    sub = lax.broadcasted_iota(jnp.int32, (GROUP, TILE), 0)
    lane = lanes(GROUP)

    def wide(v):
        return jnp.broadcast_to(v, (GROUP, TILE))

    out = []
    for own in range(count):
        first = own * GROUP
        columns = {
            g: [wide(groups[g][:, first + k : first + k + 1]) for k in range(GROUP)] for g in range(own, count)
        }
        rows = [wide(groups[own][k : k + 1, :]) for k in range(GROUP)]
        corner = [
            [wide(columns[own][m][k : k + 1, :]) if m >= k else None for m in range(GROUP)] for k in range(GROUP)
        ]
        scales = []
        for k in range(GROUP):
            scale = 1.0 / corner[k][k]
            scales.append(scale)
            for l in range(k + 1, GROUP):
                factor = corner[k][l] * scale
                rows[l] = rows[l] - factor * rows[k]
                for m in range(l, GROUP):
                    corner[l][m] = corner[l][m] - factor * corner[k][m]
        for g in range(own + 1, count):
            column = columns[g]
            for k in range(GROUP):
                factor = column[k] * scales[k]
                groups[g] = groups[g] - factor * rows[k]
                for m in range(k + 1, GROUP):
                    column[m] = column[m] - factor * corner[k][m]
        block, diagonal = rows[0], corner[0][0]
        for k in range(1, GROUP):
            block = jnp.where(sub == k, rows[k], block)
            diagonal = jnp.where(sub == k, corner[k][k], diagonal)
        out.append(jnp.where(lane >= HALF, block / jnp.sqrt(diagonal), 0.0))
    return jnp.concatenate(out, axis=0)


def unpack_square(packed):
    return jnp.concatenate([packed, swap_halves(packed)], axis=0)[:, :HALF]


def small_algebra(recv_ref, at, n_y):
    gram, projected = sum_squares(recv_ref, at, n_y)
    projected = unpack_square(projected)
    right = inverse_cholesky(gram)
    left = swap_halves(right)
    inverse = left[:, :HALF]
    rayleigh = dot(dot(inverse, projected), inverse, NT)
    mixed = right - dot(rayleigh, left)
    return left, right, mixed, rayleigh


def sum_squares(recv_ref, at, n_y):
    each = VEC // 2 // n_y
    sums = []
    for which in range(2):
        starts = [at + (2 * y + which) * each for y in range(n_y)]
        sums.append(jnp.concatenate([recv_ref[0, i : i + each, :] + recv_ref[1, i : i + each, :] for i in starts], axis=0))
    return sums


def emit_products(
    n_row, n_col, q, factor, own_gram, tiles_ref, where_ref, rows_ref, cols_ref, keep_ref, give_ref, send_y_ref,
    direct, mirrored,
):
    row_tiles, col_tiles = n_col // 2, n_row // 2
    direct[...] = jnp.zeros_like(direct)
    mirrored[...] = jnp.zeros_like(mirrored)
    cross = jnp.zeros((VEC, VEC), jnp.float32)
    for t in range(tiles_ref.shape[0]):
        i, j = rows_ref[t], cols_ref[t]
        tile = tiles_ref[t]
        row_pick = q[i]
        column_pick = q[row_tiles + j]
        product = dot(column_pick, tile, NT)
        direct[i] += product
        mirrored[j] += dot(row_pick, tile)
        cross = cross + dot(product, row_pick, NT)
    gram, projected = own_gram()
    projected = projected + factor * (cross + cross.T)
    low = lanes(VEC // 2) < HALF

    def pack_square(m):
        wide = jnp.concatenate([m, m], axis=1)
        return jnp.where(low, wide[: VEC // 2], wide[VEC // 2 :])

    n_y = send_y_ref.shape[0]
    each = VEC // 2 // n_y
    at = send_y_ref.shape[1] - 2 * each
    for which, square in enumerate((pack_square(gram), pack_square(projected))):
        for y in range(n_y):
            start = at + which * each
            send_y_ref[y, start : start + each, :] = square[y * each : (y + 1) * each]
    second = where_ref[2] == 1
    for b in range(col_tiles):
        even, odd = pack_pair(mirrored[b])
        keep_ref[b] = jnp.where(second, odd, even)
        give_ref[b] = jnp.where(second, even, odd)
    for s in range(row_tiles):
        for c, block in zip((2 * s, 2 * s + 1), pack_pair(direct[s])):
            zh, y = c // n_y, c % n_y
            send_y_ref[y, zh * (VEC // 2) : (zh + 1) * (VEC // 2), :] = block


def unpack_gathered(recv_row_ref, recv_col_ref, n_row, n_col, out):
    n_y = recv_col_ref.shape[0]
    half = VEC // 2

    def col_block(c):
        zh, y = c // n_y, c % n_y
        return recv_col_ref[y, zh * half : (zh + 1) * half, :]

    for s in range(n_col // 2):
        top, bottom = unpack_pair(col_block(2 * s), col_block(2 * s + 1))
        out[s, :half, :] = top
        out[s, half:, :] = bottom
    for b in range(n_row // 2):
        top, bottom = unpack_pair(*(recv_row_ref[core, b * half : (b + 1) * half, :] for core in range(2)))
        out[n_col // 2 + b, :half, :] = top
        out[n_col // 2 + b, half:, :] = bottom


def own_mask(where_ref):
    return (lanes(VEC) // HALF) == where_ref[1]


def first_kernel(
    n_row, n_col, where_ref, rows_ref, cols_ref, tiles_ref, recv_row_ref, recv_col_ref,
    trial_ref, keep_ref, give_ref, send_y_ref, fresh, direct, mirrored, sem,
):
    unpack_gathered(recv_row_ref, recv_col_ref, n_row, n_col, fresh)
    store = pltpu.make_async_copy(fresh, trial_ref, sem)
    store.start()

    def own_gram():
        mine = fresh[where_ref[0]]
        return dot(jnp.where(own_mask(where_ref), mine, 0.0), mine, NT), jnp.zeros((VEC, VEC), jnp.float32)

    emit_products(
        n_row, n_col, fresh, 1.0, own_gram, tiles_ref, where_ref, rows_ref, cols_ref, keep_ref, give_ref, send_y_ref,
        direct, mirrored,
    )
    store.wait()


def middle_kernel(step, n_row, n_col, *refs):
    first, last = step == 0, step == ITERS - 1
    given, stored = GIVEN[step], STORED[step]
    where_ref, rows_ref, cols_ref, tiles_ref, recv_row_ref, recv_col_ref = refs[:6]
    old_refs, refs = refs[6 : 6 + given], refs[6 + given :]
    new_refs, refs = refs[: stored or 2], refs[stored or 2 :]
    keep_ref, give_ref, send_y_ref, state, fresh, direct, mirrored, load_sems, store_sems = refs
    n_tiles = n_col // 2 + n_row // 2
    piece = n_tiles // PIECES

    def moves(outside, sems, count, inward):
        result = []
        for p in range(PIECES):
            tiles = pl.ds(p * piece, piece)
            pairs = [(outside[k].at[tiles], state.at[k, tiles]) for k in range(count)]
            result.append(
                [
                    pltpu.make_async_copy(*(pair if inward else pair[::-1]), sems.at[k, p])
                    for k, pair in enumerate(pairs)
                ]
            )
        return result

    loads = moves(old_refs, load_sems, given, True)
    stores = moves(new_refs, store_sems, stored, False)
    for part in loads:
        for load in part:
            load.start()
    trials, knowns, searches, search_images = (state.at[k] for k in range(4))
    unpack_gathered(recv_row_ref, recv_col_ref, n_row, n_col, fresh)
    left, right, mixed, _ = small_algebra(recv_row_ref, n_row // 2 * (VEC // 2), recv_col_ref.shape[0])
    coefficients = jnp.concatenate([left, right, mixed], axis=0)
    for t in range(n_tiles):
        if t % piece == 0:
            for load in loads[t // piece]:
                load.wait()
        image = fresh[t]
        trial = trials[t]
        trial_image = image if first else knowns[t] - STEP * image
        both = jnp.concatenate([trial, trial_image], axis=0)
        mixtures = dot(coefficients, both)
        basis, new_image, residual = (mixtures[VEC * k : VEC * (k + 1)] for k in range(3))
        fresh[t] = residual
        search = -STEP * residual
        if not first:
            search = search + MOMENTUM * searches[t]
            search_image = -STEP * image
            if given == 4:
                search_image = search_image + MOMENTUM * search_images[t]
            new_image = new_image + MOMENTUM * search_image
            if stored == 4:
                search_images[t] = search_image
        trials[t] = basis + search
        knowns[t] = new_image
        if not last:
            searches[t] = search
        if t % piece == piece - 1:
            for store in stores[t // piece]:
                store.start()
    if last:
        new_refs[0][...] = trials[where_ref[0]]
        new_refs[1][...] = knowns[where_ref[0]]

    def own_gram():
        at = where_ref[0]
        mask = own_mask(where_ref)
        trial = jnp.where(mask, trials[at], 0.0)
        known = jnp.where(mask, knowns[at], 0.0)
        gram = dot(trial, trial, NT)
        projected = dot(trial, known, NT) - STEP * dot(known, fresh[at], NT)
        return gram, projected

    emit_products(
        n_row, n_col, fresh, STEP * STEP, own_gram, tiles_ref, where_ref, rows_ref, cols_ref, keep_ref, give_ref,
        send_y_ref, direct, mirrored,
    )
    for part in stores:
        for store in part:
            store.wait()


def last_kernel(n_y, where_ref, recv_ref, local_ref, trial_ref, known_ref, basis_ref, rayleigh_ref, residual_ref):
    left, right, mixed, rayleigh = small_algebra(recv_ref, 0, n_y)
    block = local_ref[...]
    image = jnp.concatenate(unpack_pair(block, block), axis=0)
    trial = trial_ref[...]
    trial_image = known_ref[...] - STEP * image
    both = jnp.concatenate([trial, trial_image], axis=0)
    odd = where_ref[1] == 1
    basis = dot(left, both)
    residual = dot(mixed, both)
    basis_ref[...] = jnp.where(odd, swap_halves(basis), basis)[:, :HALF]
    residual_ref[...] = jnp.where(odd, swap_halves(residual), residual)[:, :HALF]
    rayleigh_ref[...] = rayleigh


def per_device(split, initial_block, matrix_tiles, tile_rows, tile_columns):
    n_x, n_zl, n_core, n_zh, n_y = split
    n_row, n_col = n_x * n_zl * n_core, n_zh * n_y
    n_tiles = n_row // 2 + n_col // 2
    half = VEC // 2
    sums_rows = 2 * (half // n_y)
    n_direct = n_zh * half
    tiles = matrix_tiles[0, 0]
    rows, cols = tile_rows[0, 0], tile_columns[0, 0]
    my_col = lax.axis_index("zh") * n_y + lax.axis_index("y")
    where = jnp.stack([my_col // 2, my_col % 2, lax.axis_index("core")]).astype(jnp.int32)

    smem = pl.BlockSpec(memory_space=pltpu.SMEM)
    vmem = pl.BlockSpec(memory_space=pltpu.VMEM)
    f32 = jnp.float32
    state = pltpu.HBM((n_tiles, VEC, TILE), f32)
    hbm = pl.BlockSpec(memory_space=pltpu.HBM)
    half_row = jax.ShapeDtypeStruct((n_row // 2, half, TILE), f32)
    send_y = jax.ShapeDtypeStruct((n_y, n_direct + sums_rows, TILE), f32)
    sends = (half_row, half_row, send_y)
    params = pltpu.CompilerParams(vmem_limit_bytes=20 * 1024 * 1024)
    gathered = pltpu.VMEM((n_tiles, VEC, TILE), f32)
    partial_sums = [pltpu.VMEM((n_col // 2, VEC, TILE), f32), pltpu.VMEM((n_row // 2, VEC, TILE), f32)]
    own_tile = jax.ShapeDtypeStruct((VEC, TILE), f32)

    def exchange(blocks, axes):
        return lax.all_to_all(blocks, axes, 0, 0, tiled=True)

    def spread(block, axes, count):
        return exchange(jnp.broadcast_to(block[None], (count,) + block.shape), axes)

    def reduce_row_and_y(keep, give, y_blocks):
        both_cores = keep + lax.ppermute(give, "core", [(0, 1), (1, 0)])
        along_y = jnp.sum(exchange(y_blocks, "y"), axis=0)
        sums = jnp.broadcast_to(along_y[None, n_direct:], (n_row // 2, sums_rows, TILE))
        from_chips = exchange(jnp.concatenate([both_cores, sums], axis=1), CHIPS)
        from_chips, along_y = lax.optimization_barrier((from_chips, along_y))
        return jnp.sum(from_chips, axis=0), along_y[:n_direct]

    def gather_chips(block):
        return spread(block, CHIPS, n_row // 2).reshape(n_row // 2 * half, TILE)

    def apply_and_gather(keep, give, y_blocks):
        mirrored, along_y = reduce_row_and_y(keep, give, y_blocks)
        heard = spread(jnp.concatenate([along_y, mirrored], axis=0), "zh", n_zh)
        blocks = jnp.sum(heard[:, :n_direct], axis=0).reshape(n_zh, half, TILE) + heard[:, n_direct : n_direct + half]
        sums = jnp.sum(heard[:, n_direct + half :], axis=0)
        mine = lax.dynamic_index_in_dim(blocks, lax.axis_index("zh"), 0, False)
        from_chips = gather_chips(mine)
        from_col = lax.all_gather(jnp.concatenate([blocks.reshape(n_direct, TILE), sums], axis=0), "y", axis=0)
        sums = from_col[:, n_direct:].reshape(n_y * sums_rows, TILE)
        return lax.all_gather(jnp.concatenate([from_chips, sums], axis=0), "core", axis=0), from_col

    def apply_locally(keep, give, y_blocks):
        mirrored, along_y = reduce_row_and_y(keep, give, y_blocks)
        sums = jnp.broadcast_to(mirrored[None, half:], (n_zh, sums_rows, TILE))
        blocks = along_y.reshape(n_zh, half, TILE)
        along_z = jnp.sum(exchange(jnp.concatenate([blocks, sums], axis=1), "zh"), axis=0)
        sums = spread(along_z[half:], "y", n_y).reshape(n_y * sums_rows, TILE)
        return along_z[:half] + mirrored[:half], lax.all_gather(sums, "core", axis=0)

    start = jnp.concatenate([initial_block[:half], initial_block[half:]], axis=1)
    along_z = spread(start, "zh", n_zh)
    from_chips = gather_chips(start)
    from_col = lax.all_gather(along_z.reshape(n_direct, TILE), "y", axis=0)
    from_row = lax.all_gather(from_chips, "core", axis=0)
    trial, *messages = pl.pallas_call(
        functools.partial(first_kernel, n_row, n_col),
        out_shape=(state,) + sends,
        in_specs=[smem] * 3 + [vmem] * 3,
        out_specs=(hbm,) + (vmem,) * 3,
        scratch_shapes=[gathered] + partial_sums + [pltpu.SemaphoreType.DMA],
        compiler_params=params,
    )(where, rows, cols, tiles, from_row, from_col)
    carried = [trial]
    for step in range(ITERS):
        from_row, from_col = apply_and_gather(*messages)
        stored = STORED[step]
        kept = stored or 2
        carried = [pltpu.with_memory_space_constraint(array, pltpu.HBM) for array in carried]
        results = pl.pallas_call(
            functools.partial(middle_kernel, step, n_row, n_col),
            out_shape=((state,) * stored or (own_tile,) * 2) + sends,
            in_specs=[smem] * 3 + [vmem] * 3 + [hbm] * len(carried),
            out_specs=((hbm,) * stored or (vmem,) * 2) + (vmem,) * 3,
            scratch_shapes=[pltpu.VMEM((4, n_tiles, VEC, TILE), f32), gathered]
            + partial_sums
            + [pltpu.SemaphoreType.DMA((4, PIECES)), pltpu.SemaphoreType.DMA((4, PIECES))],
            input_output_aliases={6 + k: k for k in range(min(len(carried), stored))},
            compiler_params=params,
        )(where, rows, cols, tiles, from_row, from_col, *carried)
        carried, messages = results[:kept], results[kept:]
    local, sums = apply_locally(*messages)
    small = jax.ShapeDtypeStruct((VEC, VEC), f32)
    return pl.pallas_call(
        functools.partial(last_kernel, n_y),
        out_shape=(small,) * 3,
        in_specs=[smem] + [vmem] * 4,
        out_specs=(vmem,) * 3,
        compiler_params=params,
    )(where, sums, local, *carried)


def solution(mesh, split=SPLIT):
    fine = Mesh(mesh.devices.reshape(split), AXES)
    in_specs = (
        P(None, AXES),
        P(ROW, COL, None, None, None),
        P(ROW, COL, None),
        P(ROW, COL, None),
    )
    out_specs = (P(None, AXES), P(), P(None, AXES))
    return jax.shard_map(
        functools.partial(per_device, split),
        mesh=fine,
        in_specs=in_specs,
        out_specs=out_specs,
        check_vma=False,
    )
```

```python
import functools

import jax
import jax.numpy as jnp
from jax import lax
from jax.experimental import pallas as pl
from jax.experimental.pallas import tpu as pltpu
from jax.sharding import Mesh
from jax.sharding import PartitionSpec as P

TILE = 128
HALF = 64
VEC = 64
GROUP = 8
PIECES = 4
GIVEN = (1, 3, 4, 4)
STORED = (3, 4, 4, 0)
ITERS = 4
STEP = 0.5
MOMENTUM = 0.4
AXES = ("x", "zl", "core", "zh", "y")
ROW = ("x", "zl", "core")
CHIPS = ("x", "zl")
COL = ("zh", "y")
SPLIT = (4, 4, 2, 4, 4)


def dot(a, b, contract=((1,), (0,))):
    return lax.dot_general(
        a,
        b,
        (contract, ((), ())),
        precision=lax.Precision.HIGHEST,
        preferred_element_type=jnp.float32,
    )


NT = ((1,), (1,))


def lanes(rows):
    return lax.broadcasted_iota(jnp.int32, (rows, TILE), 1)


def swap_halves(v):
    return pltpu.roll(v, HALF, 1)


def pack_pair(tile):
    low = lanes(VEC // 2) < HALF
    top, bottom = tile[: VEC // 2], tile[VEC // 2 :]
    even = jnp.where(low, top, swap_halves(bottom))
    odd = jnp.where(low, swap_halves(top), bottom)
    return even, odd


def unpack_pair(even, odd):
    low = lanes(VEC // 2) < HALF
    top = jnp.where(low, even, swap_halves(odd))
    bottom = jnp.where(low, swap_halves(even), odd)
    return top, bottom


def inverse_cholesky(packed):
    low = lanes(VEC // 2) < HALF
    row_id = lax.broadcasted_iota(jnp.int32, (VEC // 2, TILE), 0)
    col_id = lanes(VEC // 2)
    eye_top = jnp.where(col_id - HALF == row_id, 1.0, 0.0)
    eye_bottom = jnp.where(col_id - HALF == row_id + VEC // 2, 1.0, 0.0)
    top = jnp.where(low, packed, eye_top)
    bottom = jnp.where(low, swap_halves(packed), eye_bottom)
    count = VEC // GROUP
    groups = [half[GROUP * g : GROUP * (g + 1)] for half in (top, bottom) for g in range(count // 2)]
    sub = lax.broadcasted_iota(jnp.int32, (GROUP, TILE), 0)
    lane = lanes(GROUP)

    def wide(v):
        return jnp.broadcast_to(v, (GROUP, TILE))

    out = []
    for own in range(count):
        first = own * GROUP
        columns = {
            g: [wide(groups[g][:, first + k : first + k + 1]) for k in range(GROUP)] for g in range(own, count)
        }
        rows = [wide(groups[own][k : k + 1, :]) for k in range(GROUP)]
        corner = [
            [wide(columns[own][m][k : k + 1, :]) if m >= k else None for m in range(GROUP)] for k in range(GROUP)
        ]
        scales = []
        for k in range(GROUP):
            scale = 1.0 / corner[k][k]
            scales.append(scale)
            for l in range(k + 1, GROUP):
                factor = corner[k][l] * scale
                rows[l] = rows[l] - factor * rows[k]
                for m in range(l, GROUP):
                    corner[l][m] = corner[l][m] - factor * corner[k][m]
        for g in range(own + 1, count):
            column = columns[g]
            for k in range(GROUP):
                factor = column[k] * scales[k]
                groups[g] = groups[g] - factor * rows[k]
                for m in range(k + 1, GROUP):
                    column[m] = column[m] - factor * corner[k][m]
        block, diagonal = rows[0], corner[0][0]
        for k in range(1, GROUP):
            block = jnp.where(sub == k, rows[k], block)
            diagonal = jnp.where(sub == k, corner[k][k], diagonal)
        out.append(jnp.where(lane >= HALF, block / jnp.sqrt(diagonal), 0.0))
    return jnp.concatenate(out, axis=0)


def unpack_square(packed):
    return jnp.concatenate([packed, swap_halves(packed)], axis=0)[:, :HALF]


def small_algebra(recv_ref, at, n_y):
    gram, projected = sum_squares(recv_ref, at, n_y)
    projected = unpack_square(projected)
    right = inverse_cholesky(gram)
    left = swap_halves(right)
    inverse = left[:, :HALF]
    rayleigh = dot(dot(inverse, projected), inverse, NT)
    mixed = right - dot(rayleigh, left)
    return left, right, mixed, rayleigh


def sum_squares(recv_ref, at, n_y):
    each = VEC // 2 // n_y
    sums = []
    for which in range(2):
        starts = [at + (2 * y + which) * each for y in range(n_y)]
        sums.append(jnp.concatenate([recv_ref[0, i : i + each, :] + recv_ref[1, i : i + each, :] for i in starts], axis=0))
    return sums


def emit_products(
    n_row, n_col, q, factor, own_gram, tiles_ref, where_ref, rows_ref, cols_ref, keep_ref, give_ref, send_y_ref,
    direct, mirrored,
):
    row_tiles, col_tiles = n_col // 2, n_row // 2
    direct[...] = jnp.zeros_like(direct)
    mirrored[...] = jnp.zeros_like(mirrored)
    cross = jnp.zeros((VEC, VEC), jnp.float32)
    for t in range(tiles_ref.shape[0]):
        i, j = rows_ref[t], cols_ref[t]
        tile = tiles_ref[t]
        row_pick = q[i]
        column_pick = q[row_tiles + j]
        product = dot(column_pick, tile, NT)
        direct[i] += product
        mirrored[j] += dot(row_pick, tile)
        cross = cross + dot(product, row_pick, NT)
    gram, projected = own_gram()
    projected = projected + factor * (cross + cross.T)
    low = lanes(VEC // 2) < HALF

    def pack_square(m):
        wide = jnp.concatenate([m, m], axis=1)
        return jnp.where(low, wide[: VEC // 2], wide[VEC // 2 :])

    n_y = send_y_ref.shape[0]
    each = VEC // 2 // n_y
    at = send_y_ref.shape[1] - 2 * each
    for which, square in enumerate((pack_square(gram), pack_square(projected))):
        for y in range(n_y):
            start = at + which * each
            send_y_ref[y, start : start + each, :] = square[y * each : (y + 1) * each]
    second = where_ref[2] == 1
    for b in range(col_tiles):
        even, odd = pack_pair(mirrored[b])
        keep_ref[b] = jnp.where(second, odd, even)
        give_ref[b] = jnp.where(second, even, odd)
    for s in range(row_tiles):
        for c, block in zip((2 * s, 2 * s + 1), pack_pair(direct[s])):
            zh, y = c // n_y, c % n_y
            send_y_ref[y, zh * (VEC // 2) : (zh + 1) * (VEC // 2), :] = block


def unpack_gathered(recv_row_ref, recv_col_ref, n_row, n_col, out, by_chip=False):
    n_y = recv_col_ref.shape[0]
    half = VEC // 2

    def col_block(c):
        zh, y = c // n_y, c % n_y
        return recv_col_ref[y, zh * half : (zh + 1) * half, :]

    for s in range(n_col // 2):
        top, bottom = unpack_pair(col_block(2 * s), col_block(2 * s + 1))
        out[s, :half, :] = top
        out[s, half:, :] = bottom
    for b in range(n_row // 2):
        if by_chip:
            pair = [recv_row_ref[b, core * half : (core + 1) * half, :] for core in range(2)]
        else:
            pair = [recv_row_ref[core, b * half : (b + 1) * half, :] for core in range(2)]
        top, bottom = unpack_pair(*pair)
        out[n_col // 2 + b, :half, :] = top
        out[n_col // 2 + b, half:, :] = bottom


def own_mask(where_ref):
    return (lanes(VEC) // HALF) == where_ref[1]


def first_kernel(
    n_row, n_col, where_ref, rows_ref, cols_ref, tiles_ref, recv_row_ref, recv_col_ref,
    trial_ref, keep_ref, give_ref, send_y_ref, fresh, direct, mirrored, sem,
):
    unpack_gathered(recv_row_ref, recv_col_ref, n_row, n_col, fresh, by_chip=True)
    store = pltpu.make_async_copy(fresh, trial_ref, sem)
    store.start()

    def own_gram():
        mine = fresh[where_ref[0]]
        return dot(jnp.where(own_mask(where_ref), mine, 0.0), mine, NT), jnp.zeros((VEC, VEC), jnp.float32)

    emit_products(
        n_row, n_col, fresh, 1.0, own_gram, tiles_ref, where_ref, rows_ref, cols_ref, keep_ref, give_ref, send_y_ref,
        direct, mirrored,
    )
    store.wait()


def middle_kernel(step, n_row, n_col, *refs):
    first, last = step == 0, step == ITERS - 1
    given, stored = GIVEN[step], STORED[step]
    where_ref, rows_ref, cols_ref, tiles_ref, recv_row_ref, recv_col_ref = refs[:6]
    old_refs, refs = refs[6 : 6 + given], refs[6 + given :]
    new_refs, refs = refs[: stored or 2], refs[stored or 2 :]
    keep_ref, give_ref, send_y_ref, state, fresh, direct, mirrored, load_sems, store_sems = refs
    n_tiles = n_col // 2 + n_row // 2
    piece = n_tiles // PIECES

    def moves(outside, sems, count, inward):
        result = []
        for p in range(PIECES):
            tiles = pl.ds(p * piece, piece)
            pairs = [(outside[k].at[tiles], state.at[k, tiles]) for k in range(count)]
            result.append(
                [
                    pltpu.make_async_copy(*(pair if inward else pair[::-1]), sems.at[k, p])
                    for k, pair in enumerate(pairs)
                ]
            )
        return result

    loads = moves(old_refs, load_sems, given, True)
    stores = moves(new_refs, store_sems, stored, False)
    for part in loads:
        for load in part:
            load.start()
    trials, knowns, searches, search_images = (state.at[k] for k in range(4))
    unpack_gathered(recv_row_ref, recv_col_ref, n_row, n_col, fresh)
    left, right, mixed, _ = small_algebra(recv_row_ref, n_row // 2 * (VEC // 2), recv_col_ref.shape[0])
    coefficients = jnp.concatenate([left, right, mixed], axis=0)
    for t in range(n_tiles):
        if t % piece == 0:
            for load in loads[t // piece]:
                load.wait()
        image = fresh[t]
        trial = trials[t]
        trial_image = image if first else knowns[t] - STEP * image
        both = jnp.concatenate([trial, trial_image], axis=0)
        mixtures = dot(coefficients, both)
        basis, new_image, residual = (mixtures[VEC * k : VEC * (k + 1)] for k in range(3))
        fresh[t] = residual
        search = -STEP * residual
        if not first:
            search = search + MOMENTUM * searches[t]
            search_image = -STEP * image
            if given == 4:
                search_image = search_image + MOMENTUM * search_images[t]
            new_image = new_image + MOMENTUM * search_image
            if stored == 4:
                search_images[t] = search_image
        trials[t] = basis + search
        knowns[t] = new_image
        if not last:
            searches[t] = search
        if t % piece == piece - 1:
            for store in stores[t // piece]:
                store.start()
    if last:
        new_refs[0][...] = trials[where_ref[0]]
        new_refs[1][...] = knowns[where_ref[0]]

    def own_gram():
        at = where_ref[0]
        mask = own_mask(where_ref)
        trial = jnp.where(mask, trials[at], 0.0)
        known = jnp.where(mask, knowns[at], 0.0)
        gram = dot(trial, trial, NT)
        projected = dot(trial, known, NT) - STEP * dot(known, fresh[at], NT)
        return gram, projected

    emit_products(
        n_row, n_col, fresh, STEP * STEP, own_gram, tiles_ref, where_ref, rows_ref, cols_ref, keep_ref, give_ref,
        send_y_ref, direct, mirrored,
    )
    for part in stores:
        for store in part:
            store.wait()


def last_kernel(n_y, where_ref, recv_ref, local_ref, trial_ref, known_ref, basis_ref, rayleigh_ref, residual_ref):
    left, right, mixed, rayleigh = small_algebra(recv_ref, 0, n_y)
    block = local_ref[...]
    image = jnp.concatenate(unpack_pair(block, block), axis=0)
    trial = trial_ref[...]
    trial_image = known_ref[...] - STEP * image
    both = jnp.concatenate([trial, trial_image], axis=0)
    odd = where_ref[1] == 1
    basis = dot(left, both)
    residual = dot(mixed, both)
    basis_ref[...] = jnp.where(odd, swap_halves(basis), basis)[:, :HALF]
    residual_ref[...] = jnp.where(odd, swap_halves(residual), residual)[:, :HALF]
    rayleigh_ref[...] = rayleigh


def per_device(split, initial_block, matrix_tiles, tile_rows, tile_columns):
    n_x, n_zl, n_core, n_zh, n_y = split
    n_row, n_col = n_x * n_zl * n_core, n_zh * n_y
    n_tiles = n_row // 2 + n_col // 2
    half = VEC // 2
    sums_rows = 2 * (half // n_y)
    n_direct = n_zh * half
    tiles = matrix_tiles[0, 0]
    rows, cols = tile_rows[0, 0], tile_columns[0, 0]
    my_col = lax.axis_index("zh") * n_y + lax.axis_index("y")
    where = jnp.stack([my_col // 2, my_col % 2, lax.axis_index("core")]).astype(jnp.int32)

    smem = pl.BlockSpec(memory_space=pltpu.SMEM)
    vmem = pl.BlockSpec(memory_space=pltpu.VMEM)
    f32 = jnp.float32
    state = pltpu.HBM((n_tiles, VEC, TILE), f32)
    hbm = pl.BlockSpec(memory_space=pltpu.HBM)
    half_row = jax.ShapeDtypeStruct((n_row // 2, half, TILE), f32)
    send_y = jax.ShapeDtypeStruct((n_y, n_direct + sums_rows, TILE), f32)
    sends = (half_row, half_row, send_y)
    params = pltpu.CompilerParams(vmem_limit_bytes=20 * 1024 * 1024)
    gathered = pltpu.VMEM((n_tiles, VEC, TILE), f32)
    partial_sums = [pltpu.VMEM((n_col // 2, VEC, TILE), f32), pltpu.VMEM((n_row // 2, VEC, TILE), f32)]
    own_tile = jax.ShapeDtypeStruct((VEC, TILE), f32)

    def exchange(blocks, axes):
        return lax.all_to_all(blocks, axes, 0, 0, tiled=True)

    def spread(block, axes, count):
        return exchange(jnp.broadcast_to(block[None], (count,) + block.shape), axes)

    def reduce_row_and_y(keep, give, y_blocks):
        both_cores = keep + lax.ppermute(give, "core", [(0, 1), (1, 0)])
        from_y = exchange(y_blocks, "y")
        sums = jnp.sum(from_y[:, n_direct:], axis=0)
        sums = jnp.broadcast_to(sums[None], (n_row // 2, sums_rows, TILE))
        from_chips = exchange(jnp.concatenate([both_cores, sums], axis=1), CHIPS)
        from_chips, from_y = lax.optimization_barrier((from_chips, from_y))
        return jnp.sum(from_chips, axis=0), jnp.sum(from_y[:, :n_direct], axis=0)

    def gather_chips(block):
        return spread(block, CHIPS, n_row // 2).reshape(n_row // 2 * half, TILE)

    def apply_and_gather(keep, give, y_blocks):
        mirrored, along_y = reduce_row_and_y(keep, give, y_blocks)
        heard = spread(jnp.concatenate([along_y, mirrored], axis=0), "zh", n_zh)
        blocks = jnp.sum(heard[:, :n_direct], axis=0).reshape(n_zh, half, TILE) + heard[:, n_direct : n_direct + half]
        sums = jnp.sum(heard[:, n_direct + half :], axis=0)
        mine = lax.dynamic_index_in_dim(blocks, lax.axis_index("zh"), 0, False)
        from_chips = gather_chips(mine)
        from_col = lax.all_gather(jnp.concatenate([blocks.reshape(n_direct, TILE), sums], axis=0), "y", axis=0)
        sums = from_col[:, n_direct:].reshape(n_y * sums_rows, TILE)
        return lax.all_gather(jnp.concatenate([from_chips, sums], axis=0), "core", axis=0), from_col

    def apply_locally(keep, give, y_blocks):
        mirrored, along_y = reduce_row_and_y(keep, give, y_blocks)
        sums = jnp.broadcast_to(mirrored[None, half:], (n_zh, sums_rows, TILE))
        blocks = along_y.reshape(n_zh, half, TILE)
        along_z = jnp.sum(exchange(jnp.concatenate([blocks, sums], axis=1), "zh"), axis=0)
        sums = spread(along_z[half:], "y", n_y).reshape(n_y * sums_rows, TILE)
        return along_z[:half] + mirrored[:half], lax.all_gather(sums, "core", axis=0)

    start = jnp.concatenate([initial_block[:half], initial_block[half:]], axis=1)
    along_z = spread(start, "zh", n_zh)
    both_cores = lax.all_gather(start, "core", axis=0, tiled=True)
    from_row = spread(both_cores, CHIPS, n_row // 2)
    from_col = lax.all_gather(along_z.reshape(n_direct, TILE), "y", axis=0)
    trial, *messages = pl.pallas_call(
        functools.partial(first_kernel, n_row, n_col),
        out_shape=(state,) + sends,
        in_specs=[smem] * 3 + [vmem] * 3,
        out_specs=(hbm,) + (vmem,) * 3,
        scratch_shapes=[gathered] + partial_sums + [pltpu.SemaphoreType.DMA],
        compiler_params=params,
    )(where, rows, cols, tiles, from_row, from_col)
    carried = [trial]
    for step in range(ITERS):
        from_row, from_col = apply_and_gather(*messages)
        stored = STORED[step]
        kept = stored or 2
        carried = [pltpu.with_memory_space_constraint(array, pltpu.HBM) for array in carried]
        results = pl.pallas_call(
            functools.partial(middle_kernel, step, n_row, n_col),
            out_shape=((state,) * stored or (own_tile,) * 2) + sends,
            in_specs=[smem] * 3 + [vmem] * 3 + [hbm] * len(carried),
            out_specs=((hbm,) * stored or (vmem,) * 2) + (vmem,) * 3,
            scratch_shapes=[pltpu.VMEM((4, n_tiles, VEC, TILE), f32), gathered]
            + partial_sums
            + [pltpu.SemaphoreType.DMA((4, PIECES)), pltpu.SemaphoreType.DMA((4, PIECES))],
            input_output_aliases={6 + k: k for k in range(min(len(carried), stored))},
            compiler_params=params,
        )(where, rows, cols, tiles, from_row, from_col, *carried)
        carried, messages = results[:kept], results[kept:]
    local, sums = apply_locally(*messages)
    small = jax.ShapeDtypeStruct((VEC, VEC), f32)
    return pl.pallas_call(
        functools.partial(last_kernel, n_y),
        out_shape=(small,) * 3,
        in_specs=[smem] + [vmem] * 4,
        out_specs=(vmem,) * 3,
        compiler_params=params,
    )(where, sums, local, *carried)


def solution(mesh, split=SPLIT):
    fine = Mesh(mesh.devices.reshape(split), AXES)
    in_specs = (
        P(None, AXES),
        P(ROW, COL, None, None, None),
        P(ROW, COL, None),
        P(ROW, COL, None),
    )
    out_specs = (P(None, AXES), P(), P(None, AXES))
    return jax.shard_map(
        functools.partial(per_device, split),
        mesh=fine,
        in_specs=in_specs,
        out_specs=out_specs,
        check_vma=False,
    )
```

```python
import functools

import jax
import jax.numpy as jnp
from jax import lax
from jax.experimental import pallas as pl
from jax.experimental.pallas import tpu as pltpu
from jax.sharding import Mesh
from jax.sharding import PartitionSpec as P

TILE = 128
HALF = 64
VEC = 64
GROUP = 8
PIECES = 2
GIVEN = (1, 3, 4, 4)
STORED = (3, 4, 4, 0)
ITERS = 4
STEP = 0.5
MOMENTUM = 0.4
AXES = ("x", "zl", "core", "zh", "y")
ROW = ("x", "zl", "core")
CHIPS = ("x", "zl")
COL = ("zh", "y")
SPLIT = (4, 4, 2, 4, 4)


def dot(a, b, contract=((1,), (0,))):
    return lax.dot_general(
        a,
        b,
        (contract, ((), ())),
        precision=lax.Precision.HIGHEST,
        preferred_element_type=jnp.float32,
    )


NT = ((1,), (1,))


def lanes(rows):
    return lax.broadcasted_iota(jnp.int32, (rows, TILE), 1)


def swap_halves(v):
    return pltpu.roll(v, HALF, 1)


def pack_pair(tile):
    low = lanes(VEC // 2) < HALF
    top, bottom = tile[: VEC // 2], tile[VEC // 2 :]
    even = jnp.where(low, top, swap_halves(bottom))
    odd = jnp.where(low, swap_halves(top), bottom)
    return even, odd


def unpack_pair(even, odd):
    low = lanes(VEC // 2) < HALF
    top = jnp.where(low, even, swap_halves(odd))
    bottom = jnp.where(low, swap_halves(even), odd)
    return top, bottom


def inverse_cholesky(packed):
    low = lanes(VEC // 2) < HALF
    row_id = lax.broadcasted_iota(jnp.int32, (VEC // 2, TILE), 0)
    col_id = lanes(VEC // 2)
    eye_top = jnp.where(col_id - HALF == row_id, 1.0, 0.0)
    eye_bottom = jnp.where(col_id - HALF == row_id + VEC // 2, 1.0, 0.0)
    top = jnp.where(low, packed, eye_top)
    bottom = jnp.where(low, swap_halves(packed), eye_bottom)
    count = VEC // GROUP
    groups = [half[GROUP * g : GROUP * (g + 1)] for half in (top, bottom) for g in range(count // 2)]
    sub = lax.broadcasted_iota(jnp.int32, (GROUP, TILE), 0)
    lane = lanes(GROUP)

    def wide(v):
        return jnp.broadcast_to(v, (GROUP, TILE))

    out = []
    for own in range(count):
        first = own * GROUP
        columns = {
            g: [wide(groups[g][:, first + k : first + k + 1]) for k in range(GROUP)] for g in range(own, count)
        }
        rows = [wide(groups[own][k : k + 1, :]) for k in range(GROUP)]
        corner = [
            [wide(columns[own][m][k : k + 1, :]) if m >= k else None for m in range(GROUP)] for k in range(GROUP)
        ]
        scales = []
        for k in range(GROUP):
            scale = 1.0 / corner[k][k]
            scales.append(scale)
            for l in range(k + 1, GROUP):
                factor = corner[k][l] * scale
                rows[l] = rows[l] - factor * rows[k]
                for m in range(l, GROUP):
                    corner[l][m] = corner[l][m] - factor * corner[k][m]
        for g in range(own + 1, count):
            column = columns[g]
            for k in range(GROUP):
                factor = column[k] * scales[k]
                groups[g] = groups[g] - factor * rows[k]
                for m in range(k + 1, GROUP):
                    column[m] = column[m] - factor * corner[k][m]
        block, diagonal = rows[0], corner[0][0]
        for k in range(1, GROUP):
            block = jnp.where(sub == k, rows[k], block)
            diagonal = jnp.where(sub == k, corner[k][k], diagonal)
        out.append(jnp.where(lane >= HALF, block / jnp.sqrt(diagonal), 0.0))
    return jnp.concatenate(out, axis=0)


def unpack_square(packed):
    return jnp.concatenate([packed, swap_halves(packed)], axis=0)[:, :HALF]


def small_algebra(recv_ref, at, n_y):
    gram, projected = sum_squares(recv_ref, at, n_y)
    projected = unpack_square(projected)
    right = inverse_cholesky(gram)
    left = swap_halves(right)
    inverse = left[:, :HALF]
    rayleigh = dot(dot(inverse, projected), inverse, NT)
    mixed = right - dot(rayleigh, left)
    return left, right, mixed, rayleigh


def sum_squares(recv_ref, at, n_y):
    each = VEC // 2 // n_y
    sums = []
    for which in range(2):
        starts = [at + (2 * y + which) * each for y in range(n_y)]
        sums.append(jnp.concatenate([recv_ref[0, i : i + each, :] + recv_ref[1, i : i + each, :] for i in starts], axis=0))
    return sums


def emit_products(
    n_row, n_col, q, factor, own_gram, tiles_ref, where_ref, rows_ref, cols_ref, keep_ref, give_ref, send_y_ref,
    direct, mirrored,
):
    row_tiles, col_tiles = n_col // 2, n_row // 2
    direct[...] = jnp.zeros_like(direct)
    mirrored[...] = jnp.zeros_like(mirrored)
    cross = jnp.zeros((VEC, VEC), jnp.float32)
    for t in range(tiles_ref.shape[0]):
        i, j = rows_ref[t], cols_ref[t]
        tile = tiles_ref[t]
        row_pick = q[i]
        column_pick = q[row_tiles + j]
        product = dot(column_pick, tile, NT)
        direct[i] += product
        mirrored[j] += dot(row_pick, tile)
        cross = cross + dot(product, row_pick, NT)
    gram, projected = own_gram()
    projected = projected + factor * (cross + cross.T)
    low = lanes(VEC // 2) < HALF

    def pack_square(m):
        wide = jnp.concatenate([m, m], axis=1)
        return jnp.where(low, wide[: VEC // 2], wide[VEC // 2 :])

    n_y = send_y_ref.shape[0]
    each = VEC // 2 // n_y
    at = send_y_ref.shape[1] - 2 * each
    for which, square in enumerate((pack_square(gram), pack_square(projected))):
        for y in range(n_y):
            start = at + which * each
            send_y_ref[y, start : start + each, :] = square[y * each : (y + 1) * each]
    second = where_ref[2] == 1
    for b in range(col_tiles):
        even, odd = pack_pair(mirrored[b])
        keep_ref[b] = jnp.where(second, odd, even)
        give_ref[b] = jnp.where(second, even, odd)
    for s in range(row_tiles):
        for c, block in zip((2 * s, 2 * s + 1), pack_pair(direct[s])):
            zh, y = c // n_y, c % n_y
            send_y_ref[y, zh * (VEC // 2) : (zh + 1) * (VEC // 2), :] = block


def unpack_gathered(recv_row_ref, recv_col_ref, n_row, n_col, out, by_chip=False):
    n_y = recv_col_ref.shape[0]
    half = VEC // 2

    def col_block(c):
        zh, y = c // n_y, c % n_y
        return recv_col_ref[y, zh * half : (zh + 1) * half, :]

    for s in range(n_col // 2):
        top, bottom = unpack_pair(col_block(2 * s), col_block(2 * s + 1))
        out[s, :half, :] = top
        out[s, half:, :] = bottom
    for b in range(n_row // 2):
        if by_chip:
            pair = [recv_row_ref[b, core * half : (core + 1) * half, :] for core in range(2)]
        else:
            pair = [recv_row_ref[core, b * half : (b + 1) * half, :] for core in range(2)]
        top, bottom = unpack_pair(*pair)
        out[n_col // 2 + b, :half, :] = top
        out[n_col // 2 + b, half:, :] = bottom


def own_mask(where_ref):
    return (lanes(VEC) // HALF) == where_ref[1]


def first_kernel(
    n_row, n_col, where_ref, rows_ref, cols_ref, tiles_ref, recv_row_ref, recv_col_ref,
    trial_ref, keep_ref, give_ref, send_y_ref, fresh, direct, mirrored, sem,
):
    unpack_gathered(recv_row_ref, recv_col_ref, n_row, n_col, fresh, by_chip=True)
    store = pltpu.make_async_copy(fresh, trial_ref, sem)
    store.start()

    def own_gram():
        mine = fresh[where_ref[0]]
        return dot(jnp.where(own_mask(where_ref), mine, 0.0), mine, NT), jnp.zeros((VEC, VEC), jnp.float32)

    emit_products(
        n_row, n_col, fresh, 1.0, own_gram, tiles_ref, where_ref, rows_ref, cols_ref, keep_ref, give_ref, send_y_ref,
        direct, mirrored,
    )
    store.wait()


def middle_kernel(step, n_row, n_col, *refs):
    first, last = step == 0, step == ITERS - 1
    given, stored = GIVEN[step], STORED[step]
    where_ref, rows_ref, cols_ref, tiles_ref, recv_row_ref, recv_col_ref = refs[:6]
    old_refs, refs = refs[6 : 6 + given], refs[6 + given :]
    new_refs, refs = refs[: stored or 2], refs[stored or 2 :]
    keep_ref, give_ref, send_y_ref, state, fresh, direct, mirrored, load_sems, store_sems = refs
    n_tiles = n_col // 2 + n_row // 2
    piece = n_tiles // PIECES

    def moves(outside, sems, count, inward):
        result = []
        for p in range(PIECES):
            tiles = pl.ds(p * piece, piece)
            pairs = [(outside[k].at[tiles], state.at[k, tiles]) for k in range(count)]
            result.append(
                [
                    pltpu.make_async_copy(*(pair if inward else pair[::-1]), sems.at[k, p])
                    for k, pair in enumerate(pairs)
                ]
            )
        return result

    loads = moves(old_refs, load_sems, given, True)
    stores = moves(new_refs, store_sems, stored, False)
    for part in loads:
        for load in part:
            load.start()
    trials, knowns, searches, search_images = (state.at[k] for k in range(4))
    unpack_gathered(recv_row_ref, recv_col_ref, n_row, n_col, fresh)
    left, right, mixed, _ = small_algebra(recv_row_ref, n_row // 2 * (VEC // 2), recv_col_ref.shape[0])
    coefficients = jnp.concatenate([left, right, mixed], axis=0)
    for t in range(n_tiles):
        if t % piece == 0:
            for load in loads[t // piece]:
                load.wait()
        image = fresh[t]
        trial = trials[t]
        trial_image = image if first else knowns[t] - STEP * image
        both = jnp.concatenate([trial, trial_image], axis=0)
        mixtures = dot(coefficients, both)
        basis, new_image, residual = (mixtures[VEC * k : VEC * (k + 1)] for k in range(3))
        fresh[t] = residual
        search = -STEP * residual
        if not first:
            search = search + MOMENTUM * searches[t]
            search_image = -STEP * image
            if given == 4:
                search_image = search_image + MOMENTUM * search_images[t]
            new_image = new_image + MOMENTUM * search_image
            if stored == 4:
                search_images[t] = search_image
        trials[t] = basis + search
        knowns[t] = new_image
        if not last:
            searches[t] = search
        if t % piece == piece - 1:
            for store in stores[t // piece]:
                store.start()
    if last:
        new_refs[0][...] = trials[where_ref[0]]
        new_refs[1][...] = knowns[where_ref[0]]

    def own_gram():
        at = where_ref[0]
        mask = own_mask(where_ref)
        trial = jnp.where(mask, trials[at], 0.0)
        known = jnp.where(mask, knowns[at], 0.0)
        gram = dot(trial, trial, NT)
        projected = dot(
            jnp.concatenate([trial, known], axis=1), jnp.concatenate([known, -STEP * fresh[at]], axis=1), NT
        )
        return gram, projected

    emit_products(
        n_row, n_col, fresh, STEP * STEP, own_gram, tiles_ref, where_ref, rows_ref, cols_ref, keep_ref, give_ref,
        send_y_ref, direct, mirrored,
    )
    for part in stores:
        for store in part:
            store.wait()


def last_kernel(n_y, where_ref, recv_ref, local_ref, trial_ref, known_ref, basis_ref, rayleigh_ref, residual_ref):
    left, right, mixed, rayleigh = small_algebra(recv_ref, 0, n_y)
    block = local_ref[...]
    image = jnp.concatenate(unpack_pair(block, block), axis=0)
    trial = trial_ref[...]
    trial_image = known_ref[...] - STEP * image
    both = jnp.concatenate([trial, trial_image], axis=0)
    odd = where_ref[1] == 1
    basis = dot(left, both)
    residual = dot(mixed, both)
    basis_ref[...] = jnp.where(odd, swap_halves(basis), basis)[:, :HALF]
    residual_ref[...] = jnp.where(odd, swap_halves(residual), residual)[:, :HALF]
    rayleigh_ref[...] = rayleigh


def per_device(split, initial_block, matrix_tiles, tile_rows, tile_columns):
    n_x, n_zl, n_core, n_zh, n_y = split
    n_row, n_col = n_x * n_zl * n_core, n_zh * n_y
    n_tiles = n_row // 2 + n_col // 2
    half = VEC // 2
    sums_rows = 2 * (half // n_y)
    n_direct = n_zh * half
    tiles = matrix_tiles[0, 0]
    rows, cols = tile_rows[0, 0], tile_columns[0, 0]
    my_col = lax.axis_index("zh") * n_y + lax.axis_index("y")
    where = jnp.stack([my_col // 2, my_col % 2, lax.axis_index("core")]).astype(jnp.int32)

    smem = pl.BlockSpec(memory_space=pltpu.SMEM)
    vmem = pl.BlockSpec(memory_space=pltpu.VMEM)
    f32 = jnp.float32
    state = pltpu.HBM((n_tiles, VEC, TILE), f32)
    hbm = pl.BlockSpec(memory_space=pltpu.HBM)
    half_row = jax.ShapeDtypeStruct((n_row // 2, half, TILE), f32)
    send_y = jax.ShapeDtypeStruct((n_y, n_direct + sums_rows, TILE), f32)
    sends = (half_row, half_row, send_y)
    params = pltpu.CompilerParams(vmem_limit_bytes=20 * 1024 * 1024)
    gathered = pltpu.VMEM((n_tiles, VEC, TILE), f32)
    partial_sums = [pltpu.VMEM((n_col // 2, VEC, TILE), f32), pltpu.VMEM((n_row // 2, VEC, TILE), f32)]
    own_tile = jax.ShapeDtypeStruct((VEC, TILE), f32)

    def exchange(blocks, axes):
        return lax.all_to_all(blocks, axes, 0, 0, tiled=True)

    def spread(block, axes, count):
        return exchange(jnp.broadcast_to(block[None], (count,) + block.shape), axes)

    def reduce_row_and_y(keep, give, y_blocks):
        both_cores = keep + lax.ppermute(give, "core", [(0, 1), (1, 0)])
        from_y = exchange(y_blocks, "y")
        sums = jnp.sum(from_y[:, n_direct:], axis=0)
        sums = jnp.broadcast_to(sums[None], (n_row // 2, sums_rows, TILE))
        from_chips = exchange(jnp.concatenate([both_cores, sums], axis=1), CHIPS)
        from_chips, from_y = lax.optimization_barrier((from_chips, from_y))
        return jnp.sum(from_chips, axis=0), jnp.sum(from_y[:, :n_direct], axis=0)

    def gather_chips(block):
        return spread(block, CHIPS, n_row // 2).reshape(n_row // 2 * half, TILE)

    def apply_and_gather(keep, give, y_blocks):
        mirrored, along_y = reduce_row_and_y(keep, give, y_blocks)
        heard = spread(jnp.concatenate([along_y, mirrored], axis=0), "zh", n_zh)
        blocks = jnp.sum(heard[:, :n_direct], axis=0).reshape(n_zh, half, TILE) + heard[:, n_direct : n_direct + half]
        sums = jnp.sum(heard[:, n_direct + half :], axis=0)
        mine = lax.dynamic_index_in_dim(blocks, lax.axis_index("zh"), 0, False)
        from_chips = gather_chips(mine)
        from_col = lax.all_gather(jnp.concatenate([blocks.reshape(n_direct, TILE), sums], axis=0), "y", axis=0)
        sums = from_col[:, n_direct:].reshape(n_y * sums_rows, TILE)
        return lax.all_gather(jnp.concatenate([from_chips, sums], axis=0), "core", axis=0), from_col

    def apply_locally(keep, give, y_blocks):
        mirrored, along_y = reduce_row_and_y(keep, give, y_blocks)
        sums = jnp.broadcast_to(mirrored[None, half:], (n_zh, sums_rows, TILE))
        blocks = along_y.reshape(n_zh, half, TILE)
        along_z = jnp.sum(exchange(jnp.concatenate([blocks, sums], axis=1), "zh"), axis=0)
        sums = spread(along_z[half:], "y", n_y).reshape(n_y * sums_rows, TILE)
        return along_z[:half] + mirrored[:half], lax.all_gather(sums, "core", axis=0)

    start = jnp.concatenate([initial_block[:half], initial_block[half:]], axis=1)
    along_z = spread(start, "zh", n_zh)
    both_cores = lax.all_gather(start, "core", axis=0, tiled=True)
    from_row = spread(both_cores, CHIPS, n_row // 2)
    from_col = lax.all_gather(along_z.reshape(n_direct, TILE), "y", axis=0)
    trial, *messages = pl.pallas_call(
        functools.partial(first_kernel, n_row, n_col),
        out_shape=(state,) + sends,
        in_specs=[smem] * 3 + [vmem] * 3,
        out_specs=(hbm,) + (vmem,) * 3,
        scratch_shapes=[gathered] + partial_sums + [pltpu.SemaphoreType.DMA],
        compiler_params=params,
    )(where, rows, cols, tiles, from_row, from_col)
    carried = [trial]
    for step in range(ITERS):
        from_row, from_col = apply_and_gather(*messages)
        stored = STORED[step]
        kept = stored or 2
        carried = [pltpu.with_memory_space_constraint(array, pltpu.HBM) for array in carried]
        results = pl.pallas_call(
            functools.partial(middle_kernel, step, n_row, n_col),
            out_shape=((state,) * stored or (own_tile,) * 2) + sends,
            in_specs=[smem] * 3 + [vmem] * 3 + [hbm] * len(carried),
            out_specs=((hbm,) * stored or (vmem,) * 2) + (vmem,) * 3,
            scratch_shapes=[pltpu.VMEM((4, n_tiles, VEC, TILE), f32), gathered]
            + partial_sums
            + [pltpu.SemaphoreType.DMA((4, PIECES)), pltpu.SemaphoreType.DMA((4, PIECES))],
            input_output_aliases={6 + k: k for k in range(min(len(carried), stored))},
            compiler_params=params,
        )(where, rows, cols, tiles, from_row, from_col, *carried)
        carried, messages = results[:kept], results[kept:]
    local, sums = apply_locally(*messages)
    small = jax.ShapeDtypeStruct((VEC, VEC), f32)
    return pl.pallas_call(
        functools.partial(last_kernel, n_y),
        out_shape=(small,) * 3,
        in_specs=[smem] + [vmem] * 4,
        out_specs=(vmem,) * 3,
        compiler_params=params,
    )(where, sums, local, *carried)


def solution(mesh, split=SPLIT):
    fine = Mesh(mesh.devices.reshape(split), AXES)
    in_specs = (
        P(None, AXES),
        P(ROW, COL, None, None, None),
        P(ROW, COL, None),
        P(ROW, COL, None),
    )
    out_specs = (P(None, AXES), P(), P(None, AXES))
    return jax.shard_map(
        functools.partial(per_device, split),
        mesh=fine,
        in_specs=in_specs,
        out_specs=out_specs,
        check_vma=False,
    )
```
